32 devices in a mesh: expert: 8 (over y, x, core), dp: 4 (over z).
Axes of the slice: x: 2, y: 2, z: 4, core: 2. Of those that a mesh axis runs over, the one named last changes fastest.
Arguments:
- tokens: bfloat16 [4096, 2048], P(('expert', 'dp')), may hold values from -6 to 6
- cotangent: bfloat16 [4096, 2048], P(('expert', 'dp')), may hold values from -6 to 6
- gate_weights: float32 [4096, 8], P(('expert', 'dp')), may hold values from 0.02 to 0.5
- expert_ids: int32 [4096, 8], P(('expert', 'dp')), may hold values from 0 to 15, as said below
- copy_pick: int32 [4096, 8], P(('expert', 'dp')), may hold values from 0 to 1, as said below
- copy_expert: int32 [8], replicated, may hold values from 0 to 15, as said below
- up_weight: bfloat16 [16, 2048, 384], P('expert'), may hold values from -0.125 to 0.125
- down_weight: bfloat16 [16, 384, 2048], P('expert'), may hold values from -0.3125 to 0.3125
- copy_up: bfloat16 [8, 2048, 384], P('expert'), may hold values from -0.125 to 0.125
- copy_down: bfloat16 [8, 384, 2048], P('expert'), may hold values from -0.3125 to 0.3125
Outputs:
- layer_output: bfloat16 [4096, 2048], P(('expert', 'dp'))
- token_grad: bfloat16 [4096, 2048], P(('expert', 'dp'))
- gate_grad: float32 [4096, 8], P(('expert', 'dp'))
- up_grad: bfloat16 [16, 2048, 384], P('expert', 'dp')
- down_grad: bfloat16 [16, 384, 2048], P('expert', None, 'dp')
The draws below stay inside these ranges and needn't reach their ends.
Inputs may be any that keep to these rules, and one draw needn't show every extreme that they name: `expert_ids`: each row names 8 different experts. In the 128 rows of one device, the 2 experts of any one device are named 8 * 128 // 8 times together; the one of them that copy_expert lists is named at most 64 + 32 times and the other at most 64 - 32 + 32 // 2 times, and both bounds are reached in every block of rows. `copy_pick`: A 1 stands only where the pair's expert is listed in copy_expert. From the rows of one device at most 24 pairs go to one copy and at most 152 pairs go to one device (its own experts and its copy together). In each group of devices that share an index along dp, some device receives exactly 152 pairs from every device of the group, and the copy before it exactly 24 from each. `copy_expert`: entry c is one of the experts of device c - 1 along the expert axis (of the last device for entry 0); device o holds the experts 2 * o to 2 * o + 1.
All inputs are finite; a program needn't handle non-finite values.
Results may differ from the reference program's by a relative error of at most 0.014.
Values may be sent and summed in bfloat16 or wider, within the bound.
No kernel may reach another device: no remote copies, remote signals or barrier semaphores. Data moves between devices by JAX's collectives and lax.ppermute only.
A program may use at most 128 MiB of HBM per device.

```python
import math
import jax
import jax.numpy as jnp
from jax import lax

WIDTH = 2048
CHOSEN = 8
HIDDEN_SIZE = 384
LOCAL_EXPERTS = 2
TOKENS_LOCAL = 128
EXPERTS = 16
COPIES = 8
REPLICAS = 4
TOKENS = 4096
MEAN_ROWS = 64
HOT_EXTRA = 32
MOVED_MOST = 24


def routing_layout(key):
    device_count = COPIES
    block_count = COPIES * REPLICAS
    token_rows = TOKENS_LOCAL
    pair_total = token_rows * CHOSEN
    layout_key = jax.random.fold_in(key, 17)
    hot_key, surplus_key, full_key, moved_key, order_key, token_key = jax.random.split(layout_key, 6)
    hot_local = jax.random.randint(hot_key, (device_count,), 0, LOCAL_EXPERTS)
    surplus_low = HOT_EXTRA - HOT_EXTRA // 2
    surplus = jax.random.randint(surplus_key, (block_count, device_count), surplus_low, HOT_EXTRA + 1)
    block_column = jnp.arange(block_count)[:, None]
    device_index = jnp.arange(device_count)[None, :]
    surplus = jnp.where(device_index == block_column % device_count, HOT_EXTRA, surplus)
    surplus = jnp.where(device_index == (block_column + 1) % device_count, surplus_low, surplus)
    full_device = jax.random.randint(full_key, (REPLICAS,), 0, device_count)
    moved_rows = jax.random.randint(moved_key, (block_count, device_count), 0, MOVED_MOST + 1)
    block_full = full_device[jnp.arange(block_count) % REPLICAS][:, None]
    moved_rows = jnp.where(device_index == block_full, 0, moved_rows)
    moved_rows = jnp.where(device_index == (block_full + device_count - 1) % device_count, MOVED_MOST, moved_rows)
    expert_index = jnp.arange(EXPERTS)
    owner_device = expert_index // LOCAL_EXPERTS
    hot_mask = expert_index % LOCAL_EXPERTS == hot_local[owner_device]
    counts = jnp.where(hot_mask[None, :], MEAN_ROWS + surplus[:, owner_device], MEAN_ROWS - surplus[:, owner_device])
    moved_expert = jnp.where(hot_mask[None, :], moved_rows[:, owner_device], 0)
    order_keys = jax.random.split(order_key, block_count)
    token_keys = jax.random.split(token_key, block_count)

    def one_block(expert_key, shuffle_key, block_counts, block_moved):
        expert_order = jax.random.permutation(expert_key, EXPERTS)
        run_lengths = block_counts[expert_order]
        run_ends = jnp.cumsum(run_lengths)
        position = jnp.arange(pair_total)
        run_index = jnp.searchsorted(run_ends, position, side='right')
        chosen_expert = expert_order[run_index]
        run_offset = position - (run_ends[run_index] - run_lengths[run_index])
        copy_flag = (run_offset < block_moved[chosen_expert]).astype(jnp.int32)
        token_order = jax.random.permutation(shuffle_key, token_rows)
        token_slot = token_order[position % token_rows]
        column_index = position // token_rows
        chosen_ids = jnp.zeros((token_rows, CHOSEN), jnp.int32).at[token_slot, column_index].set(chosen_expert.astype(jnp.int32))
        pick_table = jnp.zeros((token_rows, CHOSEN), jnp.int32).at[token_slot, column_index].set(copy_flag)
        return (chosen_ids, pick_table)
    chosen_ids, pick_table = jax.vmap(one_block)(order_keys, token_keys, counts, moved_expert)
    previous = (jnp.arange(device_count) + device_count - 1) % device_count
    copy_table = (previous * LOCAL_EXPERTS + hot_local[previous]).astype(jnp.int32)
    return (chosen_ids.reshape(block_count * token_rows, CHOSEN), pick_table.reshape(block_count * token_rows, CHOSEN), copy_table)


def draw_expert_ids(key, part):
    return routing_layout(key)[0]


def draw_copy_pick(key, part):
    return routing_layout(key)[1]


def draw_copy_expert(key, part):
    return routing_layout(key)[2]


def level_of(key, extent, shards, least, top_value):
    def one(dim, shards_of):
        steps = jax.random.uniform(jax.random.fold_in(jax.random.fold_in(key, 6), dim), (shards_of,), jnp.float32, least / len(shards), top_value / len(shards))
        return jnp.repeat(jnp.exp(steps), extent[dim] // shards_of).reshape((-1,) + (1,) * (len(extent) - dim - 1))

    factor_of = one(*shards[0])
    for cut in shards[1:]:
        factor_of = factor_of * one(*cut)
    return factor_of


def scatter_about(own_key, shape, deviation, most, shards=(), kind=jnp.bfloat16):
    values = jax.random.normal(own_key, shape, jnp.float32) * deviation
    if len(shards) > 0:
        values = level_of(own_key, shape, shards, -0.22, 0.18) * values
    return jnp.clip(values, min=-most, max=most).astype(kind)


def setup_inputs(seed: int = 0) -> dict:
    seeds = jax.random.split(jax.random.key(seed), 11)
    tokens = scatter_about(seeds[0], (TOKENS, WIDTH), 1.0, 6.0, ((0, 32),))
    cotangent = scatter_about(seeds[1], (TOKENS, WIDTH), 1.0, 6.0, ((0, 32),))
    gate_weights = jnp.clip(jnp.exp(math.log(0.5) - 3.218876 * jax.random.uniform(seeds[2], (TOKENS, CHOSEN), jnp.float32) ** level_of(seeds[2], (TOKENS, CHOSEN), ((0, 32),), -0.2, 0.2)), 0.02, 0.5)
    expert_ids = draw_expert_ids(jax.random.fold_in(seeds[10], 71), 0)
    copy_pick = draw_copy_pick(jax.random.fold_in(seeds[10], 71), 0)
    copy_expert = draw_copy_expert(jax.random.fold_in(seeds[10], 71), 0)
    up_weight = scatter_about(seeds[6], (EXPERTS, WIDTH, HIDDEN_SIZE), WIDTH ** -0.5, 0.125, ((0, 8),))
    down_weight = scatter_about(seeds[7], (EXPERTS, HIDDEN_SIZE, WIDTH), HIDDEN_SIZE ** -0.5, 0.3125, ((0, 8),))
    copy_up = scatter_about(seeds[8], (COPIES, WIDTH, HIDDEN_SIZE), WIDTH ** -0.5, 0.125, ((0, 8),))
    copy_down = scatter_about(seeds[9], (COPIES, HIDDEN_SIZE, WIDTH), HIDDEN_SIZE ** -0.5, 0.3125, ((0, 8),))
    return dict(tokens=tokens, cotangent=cotangent, gate_weights=gate_weights, expert_ids=expert_ids, copy_pick=copy_pick, copy_expert=copy_expert, up_weight=up_weight, down_weight=down_weight, copy_up=copy_up, copy_down=copy_down)


def silu_slope(values):
    sigma_values = jax.nn.sigmoid(values)
    return sigma_values * (1.0 + values * (1.0 - sigma_values))


def rounded(values):
    return lax.optimization_barrier(values.astype(jnp.bfloat16)).astype(jnp.float32)


def expert_rows(inputs, scales, cotan_rows, weight_up, weight_down):
    linear_part = jnp.dot(inputs, weight_up, preferred_element_type=jnp.float32)
    active = jax.nn.silu(linear_part).astype(jnp.bfloat16)
    outputs = jnp.dot(active, weight_down, preferred_element_type=jnp.float32).astype(jnp.bfloat16)
    scaled = (scales[:, None] * cotan_rows.astype(jnp.float32)).astype(jnp.bfloat16)
    active_grad = jnp.dot(scaled, weight_down.T, preferred_element_type=jnp.float32)
    linear_grad = (active_grad * silu_slope(linear_part)).astype(jnp.bfloat16)
    pair_grad = jnp.dot(linear_grad, weight_up.T, preferred_element_type=jnp.float32).astype(jnp.bfloat16)
    up_part = jnp.dot(inputs.T, linear_grad, preferred_element_type=jnp.float32)
    down_part = jnp.dot(active.T, scaled, preferred_element_type=jnp.float32)
    return outputs, pair_grad, up_part, down_part


def reference(tokens, cotangent, gate_weights, expert_ids, copy_pick, copy_expert, up_weight, down_weight, copy_up, copy_down):
    group_size = COPIES * TOKENS_LOCAL
    pair_total = group_size * CHOSEN
    primary_most = COPIES * (MEAN_ROWS + HOT_EXTRA)
    copy_most = COPIES * MOVED_MOST

    def regroup(values):
        shaped = values.reshape((COPIES, REPLICAS, TOKENS_LOCAL) + values.shape[1:])
        return jnp.swapaxes(shaped, 0, 1).reshape((REPLICAS, group_size) + values.shape[1:])

    def ungroup(values):
        shaped = values.reshape((REPLICAS, COPIES, TOKENS_LOCAL) + values.shape[2:])
        return jnp.swapaxes(shaped, 0, 1).reshape((TOKENS,) + values.shape[2:])

    def one_group(totals, members):
        up_total, down_total = totals
        group_rows, group_cotan, group_gates, group_ids, group_picks = members
        flat_gates = group_gates.reshape(pair_total)
        flat_ids = group_ids.reshape(pair_total)
        flat_picks = group_picks.reshape(pair_total)

        def serve(carried, selected, most, weight_up, weight_down):
            mixed_sum, grad_sum, gate_grads = carried
            pair_index = jnp.nonzero(selected, size=most, fill_value=pair_total)[0].astype(jnp.int32)
            present = pair_index < pair_total
            clipped = jnp.minimum(pair_index, pair_total - 1)
            row_index = clipped // CHOSEN
            target_row = pair_index // CHOSEN
            inputs = jnp.where(present[:, None], group_rows[row_index], jnp.zeros((), jnp.bfloat16))
            cotan_rows = jnp.where(present[:, None], group_cotan[row_index], jnp.zeros((), jnp.bfloat16))
            scales = jnp.where(present, flat_gates[clipped], jnp.zeros((), jnp.float32))
            outputs, pair_grad, up_part, down_part = expert_rows(inputs, scales, cotan_rows, weight_up, weight_down)
            wide_out = outputs.astype(jnp.float32)
            mixed_sum = mixed_sum.at[target_row].add(scales[:, None] * wide_out, mode="drop")
            grad_sum = grad_sum.at[target_row].add(pair_grad.astype(jnp.float32), mode="drop")
            gate_grads = gate_grads.at[pair_index].set(jnp.sum(cotan_rows.astype(jnp.float32) * wide_out, axis=1), mode="drop")
            return (mixed_sum, grad_sum, gate_grads), (rounded(up_part), rounded(down_part))

        def primary(carried, expert):
            selected = (flat_ids == expert) & (flat_picks == 0)
            return serve(carried, selected, primary_most, up_weight[expert], down_weight[expert])

        def replica(carried, device):
            source = (device + COPIES - 1) % COPIES
            selected = (flat_picks == 1) & (flat_ids // LOCAL_EXPERTS == source)
            return serve(carried, selected, copy_most, copy_up[device], copy_down[device])

        initial = (jnp.zeros((group_size, WIDTH), jnp.float32), jnp.zeros((group_size, WIDTH), jnp.float32), jnp.zeros((pair_total,), jnp.float32))
        carried, (own_up, own_down) = lax.scan(primary, initial, jnp.arange(EXPERTS, dtype=jnp.int32))
        carried, (copied_up, copied_down) = lax.scan(replica, carried, jnp.arange(COPIES, dtype=jnp.int32))
        up_total = (up_total + own_up).at[copy_expert].add(copied_up)
        down_total = (down_total + own_down).at[copy_expert].add(copied_down)
        mixed_sum, grad_sum, gate_grads = carried
        return (up_total, down_total), (mixed_sum.astype(jnp.bfloat16), grad_sum.astype(jnp.bfloat16), gate_grads.reshape(group_size, CHOSEN))

    zeros_up = jnp.zeros((EXPERTS, WIDTH, HIDDEN_SIZE), jnp.float32)
    zeros_down = jnp.zeros((EXPERTS, HIDDEN_SIZE, WIDTH), jnp.float32)
    members = (regroup(tokens), regroup(cotangent), regroup(gate_weights), regroup(expert_ids), regroup(copy_pick))
    totals, (mixed_groups, grad_groups, gate_groups) = lax.scan(one_group, (zeros_up, zeros_down), members)
    return (ungroup(mixed_groups), ungroup(grad_groups), ungroup(gate_groups), totals[0].astype(jnp.bfloat16), totals[1].astype(jnp.bfloat16))
```

```python
import jax
import jax.numpy as jnp
from jax import lax
from jax.sharding import PartitionSpec as P

BF16 = jnp.bfloat16
F32 = jnp.float32


def padded(count, multiple):
    return -(-count // multiple) * multiple


def dot(a, b, contract):
    return lax.dot_general(a, b, ((contract[:1], contract[1:]), ((), ())), preferred_element_type=F32)


def split_two(values):
    high = values.astype(BF16)
    return high, (values - high.astype(F32)).astype(BF16)


class CubeExchange:
    def __init__(self):
        self.first = [(i, i ^ (4 if i & 1 else 2)) for i in range(8)]
        self.second = [(i, i ^ (2 if i & 1 else 4)) for i in range(8)]
        self.mate = [(i, i ^ 1) for i in range(8)]

    def sources(self, me):
        core = me % 2
        first = jnp.where(core == 1, 4, 2)
        second = 6 - first
        zero = jnp.zeros_like(me)
        mine = [zero, first, second, zero + 6]
        mates = [zero + 1, second + 1, first + 1, zero + 7]
        return jnp.stack([me ^ m for m in mine + mates])

    def gather(self, block):
        a = lax.ppermute(block, "expert", self.first)
        b = lax.ppermute(block, "expert", self.second)
        own_mate = lax.ppermute(block, "expert", self.mate)
        d = lax.ppermute(a, "expert", self.second)
        a_mate = lax.ppermute(a, "expert", self.mate)
        b_mate = lax.ppermute(b, "expert", self.mate)
        d_mate = lax.ppermute(d, "expert", self.mate)
        return jnp.concatenate([block, a, b, d, own_mate, a_mate, b_mate, d_mate], axis=0)

    def reduce(self, partial):
        rows = partial.shape[0] // 8
        arrived = lax.ppermute(partial[4 * rows :].astype(BF16), "expert", self.mate)
        mine = partial[: 4 * rows].astype(F32) + arrived.astype(F32)
        own, a, b, d = (mine[i * rows : (i + 1) * rows] for i in range(4))
        d_arrived = lax.ppermute(d.astype(BF16), "expert", self.second)
        b_arrived = lax.ppermute(b.astype(BF16), "expert", self.second)
        a = a + d_arrived.astype(F32)
        a_arrived = lax.ppermute(a.astype(BF16), "expert", self.first)
        return own + a_arrived.astype(F32) + b_arrived.astype(F32)


class PlainExchange:
    def __init__(self, count):
        self.count = count

    def sources(self, me):
        return jnp.arange(self.count, dtype=jnp.int32)

    def gather(self, block):
        return lax.all_gather(block, "expert", tiled=True)

    def reduce(self, partial):
        return lax.psum_scatter(
            partial.astype(BF16), "expert", scatter_dimension=0, tiled=True
        ).astype(F32)


def local(
    tokens,
    cotangent,
    gate_weights,
    expert_ids,
    copy_pick,
    copy_expert,
    up_weight,
    down_weight,
    copy_up,
    copy_down,
):
    device_count = lax.axis_size("expert")
    me = lax.axis_index("expert")
    rows, width = tokens.shape
    chosen = expert_ids.shape[1]
    local_count = up_weight.shape[0]
    hidden = up_weight.shape[2]
    expert_count = local_count * device_count
    moved_most = 3 * (rows * chosen // expert_count) // 8
    moved_rows = padded(device_count * moved_most, 128)
    exchange = CubeExchange() if device_count == 8 else PlainExchange(device_count)

    column_count = expert_count + device_count
    owner = expert_ids // local_count
    column = jnp.where(copy_pick == 1, expert_count + owner, expert_ids)
    hit = column[:, :, None] == jnp.arange(column_count, dtype=jnp.int32)
    gates = jnp.sum(jnp.where(hit, gate_weights[:, :, None], 0.0), axis=1)
    moved = jnp.sum(hit[:, :, expert_count:].astype(F32), axis=1)
    lower = (
        jnp.arange(rows, dtype=jnp.int32)[:, None] >= jnp.arange(rows, dtype=jnp.int32)[None, :]
    )
    rank = dot(lower.astype(BF16), moved.astype(BF16), (1, 0)) * moved
    gate_high, gate_low = split_two(gates)
    table_width = padded(2 * column_count + device_count, 128)
    table = jnp.concatenate(
        [
            gate_high,
            gate_low,
            rank.astype(BF16),
            jnp.zeros((rows, table_width - 2 * column_count - device_count), BF16),
        ],
        axis=1,
    )
    behind = (me + device_count - 1) % device_count
    columns = [local_count * me + i for i in range(local_count)] + [expert_count + behind]
    slots = len(columns)
    table_rows = jnp.arange(table_width, dtype=jnp.int32)
    wanted = jnp.stack(columns)
    high_pick = (table_rows[:, None] == wanted[None, :]).astype(BF16)
    low_pick = (table_rows[:, None] == wanted[None, :] + column_count).astype(BF16)
    wanted_rank = 2 * column_count + jnp.stack([behind, me])
    rank_pick = (table_rows[:, None] == wanted_rank[None, :]).astype(BF16)
    up_all = jnp.concatenate([up_weight[i] for i in range(local_count)] + [copy_up[0]], axis=1)
    down_all = jnp.concatenate(
        [down_weight[i] for i in range(local_count)] + [copy_down[0]], axis=0
    )
    to_owner = [(i, (i - 1) % device_count) for i in range(device_count)]
    hot_slot = copy_expert[(me + 1) % device_count] % local_count
    own_width = local_count * hidden

    def some_rows(own_block):
        gathered = exchange.gather(own_block)
        all_tokens = gathered[:, :width]
        all_cotangent = gathered[:, width : 2 * width]
        all_table = gathered[:, 2 * width :]
        slot_gates = dot(all_table, high_pick + low_pick, (1, 0))
        ranks = dot(all_table, rank_pick, (1, 0)).astype(jnp.int32)
        base = jnp.repeat(exchange.sources(me) * moved_most, own_block.shape[0])
        place = jnp.where(ranks > 0, base[:, None] + ranks - 1, -1)
        moved_index = jnp.arange(moved_rows, dtype=jnp.int32)[None, :]
        served_place = (place[:, :1] == moved_index).astype(BF16)
        owned_place = (place[:, 1:] == moved_index).astype(BF16)
        linear = dot(all_tokens, up_all, (1, 0))
        raw_grad = dot(all_cotangent, down_all, (1, 1))
        spread = jnp.repeat(slot_gates, hidden, axis=1)
        sigma = jax.nn.sigmoid(linear)
        active = (linear * sigma).astype(BF16).astype(F32)
        gate_part = jnp.sum((active * raw_grad).reshape(-1, slots, hidden), axis=2)
        weighted = (spread * active).astype(BF16)
        slope = sigma * (1.0 + linear * (1.0 - sigma))
        linear_grad = (spread * raw_grad * slope).astype(BF16)
        both = jnp.concatenate([linear_grad[:, own_width:], weighted[:, own_width:]], axis=1)
        packed = dot(served_place, both, (0, 0)).astype(BF16)
        packed = lax.ppermute(packed, "expert", to_owner)
        unpacked = dot(owned_place, packed, (1, 0)).astype(BF16)
        up_parts = []
        down_parts = []
        for i in range(local_count):
            here = (hot_slot == i).astype(BF16)
            part = slice(i * hidden, (i + 1) * hidden)
            total_grad = linear_grad[:, part] + unpacked[:, :hidden] * here
            total_active = weighted[:, part] + unpacked[:, hidden:] * here
            up_parts.append(dot(all_tokens, total_grad, (0, 0)))
            down_parts.append(dot(total_active, all_cotangent, (0, 0)))
        mixed = dot(weighted, down_all, (1, 0)).astype(BF16)
        back = dot(linear_grad, up_all, (1, 1)).astype(BF16)
        part_high, part_low = split_two(gate_part)
        grad_table = dot(part_high, high_pick, (1, 1)) + dot(part_low, low_pick, (1, 1))
        summed = exchange.reduce(
            jnp.concatenate([mixed, back, grad_table.astype(BF16)], axis=1)
        )
        return summed, jnp.stack(up_parts), jnp.stack(down_parts)

    own = jnp.concatenate([tokens, cotangent, table], axis=1)
    pieces = max(1, device_count // 8)
    if pieces == 1:
        summed, up_sum, down_sum = some_rows(own)
    else:

        def step(totals, piece):
            summed, up_part, down_part = some_rows(piece)
            return (totals[0] + up_part, totals[1] + down_part), summed

        zeros = (jnp.zeros(up_weight.shape, F32), jnp.zeros(down_weight.shape, F32))
        (up_sum, down_sum), summed = lax.scan(
            step, zeros, own.reshape(pieces, rows // pieces, own.shape[1])
        )
        summed = summed.reshape(rows, own.shape[1])
    up_grad = lax.psum_scatter(up_sum.astype(BF16), "dp", scatter_dimension=1, tiled=True)
    down_grad = lax.psum_scatter(down_sum.astype(BF16), "dp", scatter_dimension=2, tiled=True)
    layer_output = summed[:, :width].astype(BF16)
    token_grad = summed[:, width : 2 * width].astype(BF16)
    grads = summed[:, 2 * width : 2 * width + column_count]
    grads = grads + summed[:, 2 * width + column_count : 2 * width + 2 * column_count]
    gate_grad = jnp.sum(jnp.where(hit, grads[:, None, :], 0.0), axis=2)
    return layer_output, token_grad, gate_grad, up_grad, down_grad


def solution(mesh):
    placed = (
        P(("expert", "dp"), None),
        P(("expert", "dp"), None),
        P(("expert", "dp"), None),
        P(("expert", "dp"), None),
        P(("expert", "dp"), None),
        P(),
        P("expert", None, None),
        P("expert", None, None),
        P("expert", None, None),
        P("expert", None, None),
    )
    return jax.shard_map(
        local,
        mesh=mesh,
        in_specs=placed,
        out_specs=(
            P(("expert", "dp"), None),
            P(("expert", "dp"), None),
            P(("expert", "dp"), None),
            P("expert", "dp", None),
            P("expert", None, "dp"),
        ),
        check_vma=False,
    )
```

```python
import functools

import jax
import jax.numpy as jnp
from jax import lax
from jax.experimental import pallas as pl
from jax.experimental.pallas import tpu as pltpu
from jax.sharding import PartitionSpec as P

BF16 = jnp.bfloat16
F32 = jnp.float32


def padded(count, multiple):
    return -(-count // multiple) * multiple


def dot(a, b, contract):
    return lax.dot_general(a, b, ((contract[:1], contract[1:]), ((), ())), preferred_element_type=F32)


def split_two(values):
    high = values.astype(BF16)
    return high, (values - high.astype(F32)).astype(BF16)


VMEM_LIMIT = 64 * 1024 * 1024
ANYWHERE = pl.BlockSpec(memory_space=pl.ANY)


def call_params():
    return pltpu.CompilerParams(vmem_limit_bytes=VMEM_LIMIT)


def small_cost():
    return pl.CostEstimate(flops=1, bytes_accessed=1, transcendentals=0)


class Fetches:
    def __init__(self, sems):
        self.sems = sems
        self.copies = []

    def add(self, source, target):
        self.copies.append(
            pltpu.make_async_copy(source, target, self.sems.at[len(self.copies)])
        )
        return len(self.copies) - 1

    def start(self):
        for copy in self.copies:
            copy.start()

    def wait(self, numbers):
        for number in numbers:
            self.copies[number].wait()


COPY, COLD = "copy", "cold"
SERVED_RANK, OWNED_RANK, COLD_GATE = 3, 4, 5


def hidden_kernel(blocks, slots, packing, width, *refs):
    hot_ref, refs = refs[0], refs[1:]
    row_refs, refs = refs[:blocks], refs[blocks:]
    up_ref, down_ref, copy_up_ref, copy_down_ref, pick_ref, base_ref, *refs = refs
    before_ref = refs.pop(0) if packing == 2 else None
    grad_ref, active_ref, *refs = refs
    part_ref = refs.pop(0) if COLD not in slots else None
    place_ref, packed_ref = (refs.pop(0), refs.pop(0)) if packing else (None, None)
    together, ups, downs, gates, slot_sems, block_sems = refs
    rows = row_refs[0].shape[0]
    hidden = down_ref.shape[1]
    group = 2 * rows

    def slot_copies(number, slot):
        index = 0 if slot == COPY else (1 - hot_ref[0] if slot == COLD else slot)
        up, down = (copy_up_ref, copy_down_ref) if slot == COPY else (up_ref, down_ref)
        return [
            pltpu.make_async_copy(up.at[index], ups.at[number], slot_sems.at[number, 0]),
            pltpu.make_async_copy(down.at[index], downs.at[number], slot_sems.at[number, 1]),
        ]

    block_copies = [
        pltpu.make_async_copy(ref, together.at[pl.ds(i * rows, rows)], block_sems.at[i])
        for i, ref in enumerate(row_refs)
    ]
    for copy in slot_copies(0, slots[0]) + block_copies:
        copy.start()
    for number in range(1, len(slots)):
        for copy in slot_copies(number, slots[number]):
            copy.start()
    for copy in block_copies:
        copy.wait()
    gates[...] = dot(pick_ref[...], together[:, 2 * width :], (1, 1))
    if packing:
        ranks = gates[SERVED_RANK : OWNED_RANK + 1, :]
        place = jnp.where(ranks > 0.5, base_ref[...] + ranks - 1.0, -1.0)
        place_ref[...] = jnp.concatenate([place, jnp.zeros((6, place.shape[1]), F32)], axis=0)
    first_gate = 0 if slots[0] == COPY else (COLD_GATE if slots[0] == COLD else 1)

    @pl.loop(0, len(slots))
    def _(number):
        for copy in slot_copies(number, slots[-1]):
            copy.wait()
        to = pl.ds(pl.multiple_of(number * hidden, hidden), hidden)

        for g in range(blocks // 2):
            here = slice(g * group, (g + 1) * group)
            gate = gates[pl.ds(first_gate + number, 1), here]
            linear = dot(ups[number], together[here, :width], (0, 1))
            raw_grad = dot(downs[number], together[here, width : 2 * width], (1, 1))
            sigma = 0.5 * jnp.tanh(0.5 * linear) + 0.5
            active = (linear * sigma).astype(BF16).astype(F32)
            if part_ref is not None:
                part = jnp.sum(active * raw_grad, axis=0, keepdims=True)
                part_high, part_low = split_two(part)
                part_ref[pl.ds(pl.multiple_of(16 * number, 16), 16), here] = jnp.concatenate(
                    [part_high, part_low, jnp.zeros((14, group), BF16)], axis=0
                )
            active_ref[to, here] = (gate * active).astype(BF16)
            slope = sigma * (1.0 + linear * (1.0 - sigma))
            grad_ref[to, here] = (gate * raw_grad * slope).astype(BF16)

    if packing:
        moved_rows = packed_ref.shape[1]
        index = lax.broadcasted_iota(jnp.int32, (moved_rows, blocks * rows), 0)
        chosen = (index == place_ref[0:1, :].astype(jnp.int32)).astype(F32).astype(BF16)
        for half, ref in enumerate((grad_ref, active_ref)):
            to = slice(half * hidden, (half + 1) * hidden)
            found = dot(ref[:hidden, :], chosen, (1, 1))
            if before_ref is not None:
                found = found + before_ref[to, :].astype(F32)
            packed_ref[to, :] = found.astype(BF16)


def hidden_call(hot, blocks, weights, pick, base, slots, moved_rows=0, before=None):
    count = len(blocks)
    rows, columns = blocks[0].shape
    width, hidden = weights[0].shape[1:]
    total = count * rows
    packing = 0 if moved_rows == 0 else (1 if before is None else 2)
    vmem = pl.BlockSpec(memory_space=pltpu.VMEM)
    operands = [hot, *blocks, *weights, pick, base]
    in_specs = [pl.BlockSpec(memory_space=pltpu.SMEM)] + [ANYWHERE] * (count + 4) + [vmem] * 2
    if packing == 2:
        operands.append(before)
        in_specs.append(vmem)
    out_shape = [jax.ShapeDtypeStruct((len(slots) * hidden, total), BF16)] * 2
    if COLD not in slots:
        out_shape.append(jax.ShapeDtypeStruct((len(slots) * 16, total), BF16))
    if packing:
        out_shape.append(jax.ShapeDtypeStruct((8, total), F32))
        out_shape.append(jax.ShapeDtypeStruct((2 * hidden, moved_rows), BF16))
    return pl.pallas_call(
        functools.partial(hidden_kernel, count, slots, packing, width),
        in_specs=in_specs,
        out_specs=[vmem] * len(out_shape),
        out_shape=out_shape,
        scratch_shapes=[
            pltpu.VMEM((total, columns), BF16),
            pltpu.VMEM((len(slots), width, hidden), BF16),
            pltpu.VMEM((len(slots), hidden, width), BF16),
            pltpu.VMEM((16, total), F32),
            pltpu.SemaphoreType.DMA((len(slots), 2)),
            pltpu.SemaphoreType.DMA((count,)),
        ],
        compiler_params=call_params(),
        cost_estimate=small_cost(),
        name="hidden_units",
    )(*operands)


def fetch_pieces(fetches, pieces, expert, target):
    hidden = target.shape[0]
    found, column = [], 0
    for piece, first in pieces:
        count = piece.shape[1]
        source = piece
        if first is not None:
            start = pl.multiple_of((first + expert) * hidden, hidden)
            source = piece.at[pl.ds(start, hidden)]
        found.append(fetches.add(source, target.at[:, pl.ds(column, count)]))
        column += count
    return found


def chunk_copies_of(row_refs, tokens, cotan, width, sems):
    rows, chunk = row_refs[0].shape[0], tokens.shape[2]

    def copies(place, number, half):
        columns = pl.ds(pl.multiple_of(half * width + number * chunk, chunk), chunk)
        target = (tokens, cotan)[half]
        return [
            pltpu.make_async_copy(
                ref.at[:, columns],
                target.at[place, pl.ds(i * rows, rows)],
                sems.at[place, half, i],
            )
            for i, ref in enumerate(row_refs)
        ]

    return copies


def hot_kernel(blocks, firsts, width, *refs):
    hot_ref, refs = refs[0], refs[1:]
    row_refs, refs = refs[:blocks], refs[blocks:]
    pieces = len(firsts)
    grad_refs, active_refs, place_refs, refs = (
        refs[:pieces], refs[pieces : 2 * pieces], refs[2 * pieces : 3 * pieces], refs[3 * pieces :]
    )
    packed_ref, out_ref, grads, actives, tokens, cotan, sems, chunk_sems = refs
    chunks, total, chunk = tokens.shape
    hidden = grads.shape[0]
    fetches = Fetches(sems)
    of_rows = []
    for sources, target in ((grad_refs, grads), (active_refs, actives)):
        of_rows.append(fetch_pieces(fetches, list(zip(sources, firsts)), hot_ref[0], target))
    chunk_copies = chunk_copies_of(row_refs, tokens, cotan, width, chunk_sems)
    fetches.start()

    @pl.loop(0, chunks)
    def _(j):
        for copy in chunk_copies(j, j, 0) + chunk_copies(j, j, 1):
            copy.start()

    place = jnp.concatenate([ref[1:2, :] for ref in place_refs], axis=1)
    index = lax.broadcasted_iota(jnp.int32, (packed_ref.shape[1], total), 0)
    chosen = (index == place.astype(jnp.int32)).astype(F32).astype(BF16)
    for half, target in enumerate((grads, actives)):
        fetches.wait(of_rows[half])
        spread = dot(packed_ref[half * hidden : (half + 1) * hidden, :], chosen, (1, 0))
        target[...] = (target[...].astype(F32) + spread).astype(BF16)

    @pl.loop(0, chunks)
    def _(j):
        for half, (left, right) in enumerate(((grads, tokens), (actives, cotan))):
            for copy in chunk_copies(j, j, half):
                copy.wait()
            out_ref[j, half] = dot(left[...], right[j], (1, 0)).astype(BF16)


def hot_call(hot, blocks, firsts, grads, actives, places, packed, width, chunks):
    count = len(blocks)
    total = count * blocks[0].shape[0]
    chunk = width // chunks
    hidden = packed.shape[0] // 2
    vmem = pl.BlockSpec(memory_space=pltpu.VMEM)
    return pl.pallas_call(
        functools.partial(hot_kernel, count, firsts, width),
        in_specs=[pl.BlockSpec(memory_space=pltpu.SMEM)]
        + [ANYWHERE] * (count + 2 * len(firsts))
        + [vmem] * (len(firsts) + 1),
        out_specs=vmem,
        out_shape=jax.ShapeDtypeStruct((chunks, 2, hidden, chunk), BF16),
        scratch_shapes=[
            pltpu.VMEM((hidden, total), BF16),
            pltpu.VMEM((hidden, total), BF16),
            pltpu.VMEM((chunks, total, chunk), BF16),
            pltpu.VMEM((chunks, total, chunk), BF16),
            pltpu.SemaphoreType.DMA((2 * len(firsts),)),
            pltpu.SemaphoreType.DMA((chunks, 2, count)),
        ],
        compiler_params=call_params(),
        cost_estimate=small_cost(),
        name="hot_weight_grads",
    )(hot, *blocks, *grads, *actives, *places, packed)


def cold_kernel(blocks, firsts, width, *refs):
    hot_ref, chunk_ref, refs = refs[0], refs[1], refs[2:]
    row_refs, refs = refs[:blocks], refs[blocks:]
    pieces = len(firsts)
    grad_refs, active_refs, refs = refs[:pieces], refs[pieces : 2 * pieces], refs[2 * pieces :]
    near_ref, far_ref, grads, actives, tokens, cotan, sems, chunk_sems = refs
    fetches = Fetches(sems)
    of_rows = []
    for sources, target in ((grad_refs, grads), (active_refs, actives)):
        of_rows.append(fetch_pieces(fetches, list(zip(sources, firsts)), 1 - hot_ref[0], target))
    chunk_copies = chunk_copies_of(row_refs, tokens, cotan, width, chunk_sems)
    fetches.start()

    @pl.loop(0, 2)
    def _(j):
        for copy in chunk_copies(j, chunk_ref[j], 0) + chunk_copies(j, chunk_ref[j], 1):
            copy.start()

    for j, out_ref in enumerate((near_ref, far_ref)):
        for half, (left, right) in enumerate(((grads, tokens), (actives, cotan))):
            if j == 0:
                fetches.wait(of_rows[half])
            for copy in chunk_copies(j, chunk_ref[j], half):
                copy.wait()
            out_ref[half] = dot(left[...], right[j], (1, 0)).astype(BF16)


def cold_call(hot, chunk_pair, blocks, firsts, grads, actives, width, chunk):
    count = len(blocks)
    total = count * blocks[0].shape[0]
    hidden = grads[-1].shape[0]
    vmem = pl.BlockSpec(memory_space=pltpu.VMEM)
    smem = pl.BlockSpec(memory_space=pltpu.SMEM)
    return pl.pallas_call(
        functools.partial(cold_kernel, count, firsts, width),
        in_specs=[smem, smem] + [ANYWHERE] * (count + 2 * len(firsts)),
        out_specs=[vmem, vmem],
        out_shape=[jax.ShapeDtypeStruct((2, hidden, chunk), BF16)] * 2,
        scratch_shapes=[
            pltpu.VMEM((hidden, total), BF16),
            pltpu.VMEM((hidden, total), BF16),
            pltpu.VMEM((2, total, chunk), BF16),
            pltpu.VMEM((2, total, chunk), BF16),
            pltpu.SemaphoreType.DMA((2 * len(firsts),)),
            pltpu.SemaphoreType.DMA((2, 2, count)),
        ],
        compiler_params=call_params(),
        cost_estimate=small_cost(),
        name="cold_weight_grads",
    )(hot, chunk_pair, *blocks, *grads, *actives)


def rows_kernel(half, pieces, is_output, with_arrived, *refs):
    left_refs, refs = refs[:pieces], refs[pieces:]
    own_ref, copy_ref, *refs = refs
    part_refs, pick_ref = (), None
    if is_output:
        part_refs, pick_ref, refs = refs[:pieces], refs[pieces], refs[pieces + 1 :]
    arrived_ref = refs.pop(0) if with_arrived else None
    outs = 4 if with_arrived else 1
    out_refs, refs = refs[:outs], refs[outs:]
    left, weights, out, *refs = refs
    arrived = refs.pop(0) if with_arrived else None
    sems, chunk_sems, out_sems = refs
    hidden = own_ref.shape[1] if is_output else own_ref.shape[2]
    width = own_ref.shape[2] if is_output else own_ref.shape[1]
    step = weights.shape[3] if is_output else weights.shape[2]
    chunks = width // step
    slots = weights.shape[1]
    fetches = Fetches(sems)
    of_left = []
    row, column = 0, 0
    for ref in left_refs:
        count = ref.shape[1] // 2
        of_left.append(
            fetches.add(
                ref.at[:, pl.ds(half * count, count)],
                left.at[pl.ds(row, ref.shape[0]), pl.ds(column, count)],
            )
        )
        row += ref.shape[0]
        if row == left.shape[0]:
            row, column = 0, column + count
    fetches.start()
    tail = pl.ds(width, out.shape[1] - width)

    def chunk_copies(j):
        here = pl.ds(pl.multiple_of(j * step, step), step)
        found = []
        for slot in range(slots):
            source = copy_ref.at[0] if slot == 0 else own_ref.at[slot - 1]
            source = source.at[:, here] if is_output else source.at[here]
            found.append(
                pltpu.make_async_copy(source, weights.at[j, slot], chunk_sems.at[j, slot])
            )
        if with_arrived:
            found.append(
                pltpu.make_async_copy(
                    arrived_ref.at[:, here], arrived.at[:, here], chunk_sems.at[j, slots]
                )
            )
        return found

    def stores_of(here, number):
        rows = out.shape[0] // outs
        return [
            pltpu.make_async_copy(
                out.at[pl.ds(i * rows, rows), here], ref.at[:, here], out_sems.at[number, i]
            )
            for i, ref in enumerate(out_refs)
        ]

    tail_copies = []
    if with_arrived and is_output:
        tail_copies.append(
            pltpu.make_async_copy(
                arrived_ref.at[:, tail], arrived.at[:, tail], chunk_sems.at[chunks, 0]
            )
        )

    @pl.loop(0, chunks)
    def _(j):
        for copy in chunk_copies(j):
            copy.start()

    for copy in tail_copies:
        copy.start()
    fetches.wait(of_left)

    def store(here, number, values):
        if with_arrived:
            values = values + arrived[:, here].astype(F32)
        out[:, here] = values.astype(BF16)
        for copy in stores_of(here, number):
            copy.start()

    @pl.loop(0, chunks)
    def _(j):
        here = pl.ds(pl.multiple_of(j * step, step), step)
        for copy in chunk_copies(j):
            copy.wait()
        if is_output:
            right = weights[j].reshape(slots * hidden, step)
            values = dot(left[...], right, (0, 0))
        else:
            right = jnp.concatenate([weights[j, slot] for slot in range(slots)], axis=1)
            values = dot(left[...], right, (0, 1))
        store(here, j, values)

    if is_output:
        tables, stacked = [], []
        for ref in part_refs:
            count = ref.shape[1] // 2
            stacked.append(ref[:, half * count : (half + 1) * count])
            if sum(values.shape[0] for values in stacked) == pick_ref.shape[0]:
                tables.append(jnp.concatenate(stacked, axis=0))
                stacked = []
        table = jnp.concatenate(tables, axis=1)
        for copy in tail_copies:
            copy.wait()
        store(tail, chunks, dot(table, pick_ref[...], (0, 0)))

    @pl.loop(0, chunks)
    def _(j):
        for copy in stores_of(pl.ds(pl.multiple_of(j * step, step), step), j):
            copy.wait()

    if is_output:
        for copy in stores_of(tail, chunks):
            copy.wait()


def rows_call(half, lefts, own, copied, parts=None, pick=None, arrived=None):
    is_output = parts is not None
    slots = own.shape[0] + 1
    width, hidden = (own.shape[2], own.shape[1]) if is_output else own.shape[1:]
    total = sum(a.shape[1] * a.shape[0] for a in lefts) // (2 * slots * hidden)
    columns = width + (pick.shape[1] if is_output else 0)
    step = 512
    chunks = width // step
    vmem = pl.BlockSpec(memory_space=pltpu.VMEM)
    operands = [*lefts, own, copied]
    in_specs = [ANYWHERE] * len(operands)
    if is_output:
        operands += [*parts, pick]
        in_specs += [vmem] * (len(parts) + 1)
    scratch = [
        pltpu.VMEM((slots * hidden, total), BF16),
        pltpu.VMEM((chunks, slots) + ((hidden, step) if is_output else (step, hidden)), BF16),
        pltpu.VMEM((total, columns), BF16),
    ]
    if arrived is not None:
        operands.append(arrived)
        in_specs.append(ANYWHERE)
        scratch.append(pltpu.VMEM((total, columns), BF16))
    scratch.append(pltpu.SemaphoreType.DMA((len(lefts),)))
    scratch.append(pltpu.SemaphoreType.DMA((chunks + 1, slots + 1)))
    outs = 1 if arrived is None else 4
    scratch.append(pltpu.SemaphoreType.DMA((chunks + 1, outs)))
    return pl.pallas_call(
        functools.partial(rows_kernel, half, len(lefts), is_output, arrived is not None),
        in_specs=in_specs,
        out_specs=[ANYWHERE] * outs,
        out_shape=[jax.ShapeDtypeStruct((total // outs, columns), BF16)] * outs,
        scratch_shapes=scratch,
        compiler_params=call_params(),
        cost_estimate=small_cost(),
        name="output_rows" if is_output else "gradient_rows",
    )(*operands)


class CubeExchange:
    def __init__(self):
        self.first = [(i, i ^ (4 if i & 1 else 2)) for i in range(8)]
        self.second = [(i, i ^ (2 if i & 1 else 4)) for i in range(8)]
        self.mate = [(i, i ^ 1) for i in range(8)]

    def sources(self, me):
        first = jnp.where(me % 2 == 1, 4, 2)
        second = 6 - first
        zero = jnp.zeros_like(me)
        return me ^ jnp.stack(
            [zero, zero + 1, first, second, second + 1, first + 1, zero + 6, zero + 7]
        )

    def first_hop(self, block):
        return lax.ppermute(block, "expert", self.first)

    def far(self, first_block):
        return lax.ppermute(first_block, "expert", self.second)

    def to_mate(self, block):
        return lax.ppermute(block, "expert", self.mate)

    def reduce(self, blocks, before_last):
        own, a, b, d = blocks
        d_arrived = lax.ppermute(d, "expert", self.second)
        b_arrived = lax.ppermute(b, "expert", self.second)
        d_arrived, _ = lax.optimization_barrier((d_arrived, before_last))
        a = (a.astype(F32) + d_arrived.astype(F32)).astype(BF16)
        a_arrived = lax.ppermute(a, "expert", self.first)
        return own.astype(F32) + a_arrived.astype(F32) + b_arrived.astype(F32)


class PlainExchange:
    def __init__(self, count):
        self.count = count

    def sources(self, me):
        return jnp.arange(self.count, dtype=jnp.int32)

    def gather(self, block):
        return lax.all_gather(block, "expert", tiled=True)

    def reduce(self, partial):
        return lax.psum_scatter(
            partial.astype(BF16), "expert", scatter_dimension=0, tiled=True
        ).astype(F32)


def local(
    tokens,
    cotangent,
    gate_weights,
    expert_ids,
    copy_pick,
    copy_expert,
    up_weight,
    down_weight,
    copy_up,
    copy_down,
):
    device_count = lax.axis_size("expert")
    me = lax.axis_index("expert")
    rows, width = tokens.shape
    chosen = expert_ids.shape[1]
    local_count = up_weight.shape[0]
    hidden = up_weight.shape[2]
    expert_count = local_count * device_count
    moved_most = 3 * (rows * chosen // expert_count) // 8
    moved_rows = padded(device_count * moved_most, 128)

    column_count = expert_count + device_count
    owner = expert_ids // local_count
    column = jnp.where(copy_pick == 1, expert_count + owner, expert_ids)
    hit = column[:, :, None] == jnp.arange(column_count, dtype=jnp.int32)
    gates = jnp.sum(jnp.where(hit, gate_weights[:, :, None], 0.0), axis=1)
    moved = jnp.sum(hit[:, :, expert_count:].astype(F32), axis=1)
    lower = (
        jnp.arange(rows, dtype=jnp.int32)[:, None] >= jnp.arange(rows, dtype=jnp.int32)[None, :]
    )
    rank = dot(lower.astype(BF16), moved.astype(BF16), (1, 0)) * moved
    gate_high, gate_low = split_two(gates)
    table_width = padded(2 * column_count + device_count, 128)
    table = jnp.concatenate(
        [
            gate_high,
            gate_low,
            rank.astype(BF16),
            jnp.zeros((rows, table_width - 2 * column_count - device_count), BF16),
        ],
        axis=1,
    )
    behind = (me + device_count - 1) % device_count
    columns = [local_count * me + i for i in range(local_count)] + [expert_count + behind]
    slots = len(columns)
    table_rows = jnp.arange(table_width, dtype=jnp.int32)
    wanted = jnp.stack(columns)
    high_pick = (table_rows[:, None] == wanted[None, :]).astype(BF16)
    low_pick = (table_rows[:, None] == wanted[None, :] + column_count).astype(BF16)
    wanted_rank = 2 * column_count + jnp.stack([behind, me])
    rank_pick = (table_rows[:, None] == wanted_rank[None, :]).astype(BF16)
    to_owner = [(i, (i - 1) % device_count) for i in range(device_count)]
    hot_slot = copy_expert[(me + 1) % device_count] % local_count
    own_width = local_count * hidden

    def finish(output_sum, gradient_sum, table_sum):
        grads = table_sum[:, :column_count] + table_sum[:, column_count : 2 * column_count]
        gate_grad = jnp.sum(jnp.where(hit, grads[:, None, :], 0.0), axis=2)
        return output_sum.astype(BF16), gradient_sum.astype(BF16), gate_grad

    replicas = lax.axis_size("dp")
    if device_count == 8 and local_count == 2 and replicas == 4:
        exchange = CubeExchange()
        replica = lax.axis_index("dp")
        hot = hot_slot.reshape(1).astype(jnp.int32)
        cold_column = local_count * me + 1 - hot_slot
        weights = (up_weight, down_weight, copy_up, copy_down)
        base = jnp.repeat((exchange.sources(me) * moved_most).astype(F32), rows)[None, :]
        slot_columns = jnp.stack([wanted[slots - 1], wanted[0], wanted[1]])
        pick_columns = jnp.stack(
            [wanted[slots - 1], wanted[0], wanted[1], wanted_rank[0], wanted_rank[1], cold_column]
            + [jnp.int32(-1)] * 10
        )
        is_gate = jnp.array([1, 1, 1, 0, 0, 1] + [0] * 10, jnp.int32)
        pick = (
            (table_rows[None, :] == pick_columns[:, None])
            | (
                (table_rows[None, :] == pick_columns[:, None] + column_count)
                & (is_gate[:, None] == 1)
            )
        ).astype(BF16)
        part_columns = jnp.stack(
            [slot_columns, slot_columns + column_count] + [jnp.full((slots,), -1, jnp.int32)] * 14,
            axis=1,
        ).reshape(-1)
        part_pick = (table_rows[None, :] == part_columns[:, None]).astype(BF16)

        own = jnp.concatenate([tokens, cotangent, table], axis=1)
        own_mate = exchange.to_mate(own)
        a, b = exchange.first_hop(own), exchange.far(own)
        replica_pairs = [(0, 1), (1, 0), (2, 3), (3, 2)]
        other = lax.ppermute(own, "dp", replica_pairs)
        blocks_1 = [own, own_mate]
        ends = (2 * rows, 6 * rows)
        grad_1, active_1, part_1, place_1, packed = hidden_call(
            hot, blocks_1, weights, pick, base[:, : ends[0]], (COPY, 0, 1), moved_rows
        )
        a, b, grad_1 = lax.optimization_barrier((a, b, grad_1))
        d = exchange.far(a)
        a_mate = exchange.to_mate(a)
        other, a_mate = lax.optimization_barrier((other, a_mate))
        blocks_2 = [a, b, a_mate, exchange.to_mate(b)]
        grad_2, active_2, part_2, place_2, packed = hidden_call(
            hot, blocks_2, weights, pick, base[:, ends[0] : ends[1]], (COPY, 0, 1), moved_rows,
            packed,
        )
        grad_2, d = lax.optimization_barrier((grad_2, d))
        blocks_3 = [d, exchange.to_mate(d)]
        blocks = blocks_1 + blocks_2 + blocks_3

        other_a = exchange.first_hop(other)

        late_base = base[:, ends[1] :]
        grad_copy, active_copy, part_copy, place_3, packed = hidden_call(
            hot, blocks_3, weights, pick, late_base, (COPY,), moved_rows, packed
        )
        packed = lax.ppermute(packed, "expert", to_owner)
        grad_3, active_3, part_3 = hidden_call(hot, blocks_3, weights, pick, late_base, (0, 1))
        packed, grad_3, other, other_a = lax.optimization_barrier(
            (packed, grad_3, other, other_a)
        )
        other_b = exchange.far(other)
        other_d = exchange.far(other_a)
        hot_grads = hot_call(
            hot, blocks, (1, 1, 0), (grad_1, grad_2, grad_3), (active_1, active_2, active_3),
            (place_1, place_2, place_3), packed, width, replicas,
        )
        hot_sum = lax.psum_scatter(hot_grads, "dp", scatter_dimension=0, tiled=True)[0]

        grad_3, active_3, other_b, _ = lax.optimization_barrier(
            (grad_3, active_3, other_b, hot_grads)
        )
        outputs = ((active_1, active_2, active_copy, active_3), down_weight, copy_down)
        output_parts = ((part_1, part_2, part_copy, part_3), part_pick)
        gradients = ((grad_1, grad_2, grad_copy, grad_3), up_weight, copy_up)
        (mates_gradient,) = rows_call(1, *gradients)
        active_3, other_d, _ = lax.optimization_barrier((active_3, other_d, mates_gradient))
        outputs = ((active_1, active_2, active_copy, active_3), down_weight, copy_down)
        (mates_output,) = rows_call(1, *outputs, *output_parts)
        arrived_gradient = exchange.to_mate(mates_gradient)
        arrived_output = exchange.to_mate(mates_output)

        pair_blocks = [other, other_a, other_b, other_d]
        pair_blocks = pair_blocks + [exchange.to_mate(block) for block in pair_blocks]
        gradient_rows = rows_call(0, *gradients, None, None, arrived_gradient)
        *pair_blocks, arrived_output, _ = lax.optimization_barrier(
            (*pair_blocks, arrived_output, gradient_rows[0])
        )
        output_rows = rows_call(0, *outputs, *output_parts, arrived_output)

        *pair_blocks, _, _ = lax.optimization_barrier((*pair_blocks, gradient_rows[0], output_rows[0]))
        grad_pair, active_pair = hidden_call(hot, pair_blocks, weights, pick, base, (COLD,))
        even = replica % 2 == 0
        chunk_pair = jnp.where(even, jnp.array([1, 0]), jnp.array([2, 3])).astype(jnp.int32)
        near, far = cold_call(
            hot, chunk_pair, blocks + pair_blocks, (1, 1, 0, None),
            (grad_1, grad_2, grad_3, grad_pair), (active_1, active_2, active_3, active_pair),
            width, width // replicas,
        )
        gradient_sum = exchange.reduce(gradient_rows, near)
        output_sum = exchange.reduce(output_rows, near)
        over = lax.ppermute(far, "dp", [(1, 3), (2, 0)])
        over, across = lax.optimization_barrier((over, near))
        across = lax.ppermute(across, "dp", [(1, 2), (2, 1)])
        inward = lax.ppermute(near, "dp", [(0, 1), (3, 2)])
        at_end = (replica == 0) | (replica == replicas - 1)
        kept = jnp.where(at_end, far, jnp.zeros((), BF16))
        cold_sum = (
            across.astype(F32) + over.astype(F32) + inward.astype(F32) + kept.astype(F32)
        ).astype(BF16)
        hot_first = hot_slot == 0
        both = jnp.stack(
            [jnp.where(hot_first, hot_sum, cold_sum), jnp.where(hot_first, cold_sum, hot_sum)]
        )
        up_grad = jnp.swapaxes(both[:, 0], 1, 2)
        down_grad = both[:, 1]
        return (*finish(output_sum[:, :width], gradient_sum, output_sum[:, width:]), up_grad, down_grad)

    exchange = PlainExchange(device_count)
    up_all = jnp.concatenate([up_weight[i] for i in range(local_count)] + [copy_up[0]], axis=1)
    down_all = jnp.concatenate(
        [down_weight[i] for i in range(local_count)] + [copy_down[0]], axis=0
    )

    def some_rows(own_block):
        gathered = exchange.gather(own_block)
        all_tokens = gathered[:, :width]
        all_cotangent = gathered[:, width : 2 * width]
        all_table = gathered[:, 2 * width :]
        slot_gates = dot(all_table, high_pick + low_pick, (1, 0))
        ranks = dot(all_table, rank_pick, (1, 0)).astype(jnp.int32)
        base = jnp.repeat(exchange.sources(me) * moved_most, own_block.shape[0])
        place = jnp.where(ranks > 0, base[:, None] + ranks - 1, -1)
        moved_index = jnp.arange(moved_rows, dtype=jnp.int32)[None, :]
        served_place = (place[:, :1] == moved_index).astype(BF16)
        owned_place = (place[:, 1:] == moved_index).astype(BF16)
        linear = dot(all_tokens, up_all, (1, 0))
        raw_grad = dot(all_cotangent, down_all, (1, 1))
        spread = jnp.repeat(slot_gates, hidden, axis=1)
        sigma = jax.nn.sigmoid(linear)
        active = (linear * sigma).astype(BF16).astype(F32)
        gate_part = jnp.sum((active * raw_grad).reshape(-1, slots, hidden), axis=2)
        weighted = (spread * active).astype(BF16)
        slope = sigma * (1.0 + linear * (1.0 - sigma))
        linear_grad = (spread * raw_grad * slope).astype(BF16)
        both = jnp.concatenate([linear_grad[:, own_width:], weighted[:, own_width:]], axis=1)
        packed = dot(served_place, both, (0, 0)).astype(BF16)
        packed = lax.ppermute(packed, "expert", to_owner)
        unpacked = dot(owned_place, packed, (1, 0)).astype(BF16)
        up_parts = []
        down_parts = []
        for i in range(local_count):
            here = (hot_slot == i).astype(BF16)
            part = slice(i * hidden, (i + 1) * hidden)
            total_grad = linear_grad[:, part] + unpacked[:, :hidden] * here
            total_active = weighted[:, part] + unpacked[:, hidden:] * here
            up_parts.append(dot(all_tokens, total_grad, (0, 0)))
            down_parts.append(dot(total_active, all_cotangent, (0, 0)))
        mixed = dot(weighted, down_all, (1, 0)).astype(BF16)
        back = dot(linear_grad, up_all, (1, 1)).astype(BF16)
        part_high, part_low = split_two(gate_part)
        grad_table = dot(part_high, high_pick, (1, 1)) + dot(part_low, low_pick, (1, 1))
        summed = exchange.reduce(
            jnp.concatenate([mixed, back, grad_table.astype(BF16)], axis=1)
        )
        return summed, jnp.stack(up_parts), jnp.stack(down_parts)

    own = jnp.concatenate([tokens, cotangent, table], axis=1)
    pieces = max(1, device_count // 8)
    if pieces == 1:
        summed, up_sum, down_sum = some_rows(own)
    else:

        def step(totals, piece):
            summed, up_part, down_part = some_rows(piece)
            return (totals[0] + up_part, totals[1] + down_part), summed

        zeros = (jnp.zeros(up_weight.shape, F32), jnp.zeros(down_weight.shape, F32))
        (up_sum, down_sum), summed = lax.scan(
            step, zeros, own.reshape(pieces, rows // pieces, own.shape[1])
        )
        summed = summed.reshape(rows, own.shape[1])
    up_grad = lax.psum_scatter(up_sum.astype(BF16), "dp", scatter_dimension=1, tiled=True)
    down_grad = lax.psum_scatter(down_sum.astype(BF16), "dp", scatter_dimension=2, tiled=True)
    parts = (summed[:, :width], summed[:, width : 2 * width], summed[:, 2 * width :])
    return (*finish(*parts), up_grad, down_grad)


def solution(mesh):
    placed = (
        P(("expert", "dp"), None),
        P(("expert", "dp"), None),
        P(("expert", "dp"), None),
        P(("expert", "dp"), None),
        P(("expert", "dp"), None),
        P(),
        P("expert", None, None),
        P("expert", None, None),
        P("expert", None, None),
        P("expert", None, None),
    )
    return jax.shard_map(
        local,
        mesh=mesh,
        in_specs=placed,
        out_specs=(
            P(("expert", "dp"), None),
            P(("expert", "dp"), None),
            P(("expert", "dp"), None),
            P("expert", "dp", None),
            P("expert", None, "dp"),
        ),
        check_vma=False,
    )
```

```python
import functools

import jax
import jax.numpy as jnp
from jax import lax
from jax.experimental import pallas as pl
from jax.experimental.pallas import tpu as pltpu
from jax.sharding import PartitionSpec as P

BF16 = jnp.bfloat16
F32 = jnp.float32


def padded(count, multiple):
    return -(-count // multiple) * multiple


def dot(a, b, contract):
    return lax.dot_general(a, b, ((contract[:1], contract[1:]), ((), ())), preferred_element_type=F32)


def split_two(values):
    high = values.astype(BF16)
    return high, (values - high.astype(F32)).astype(BF16)


VMEM_LIMIT = 64 * 1024 * 1024
ANYWHERE = pl.BlockSpec(memory_space=pl.ANY)


def call_params():
    return pltpu.CompilerParams(vmem_limit_bytes=VMEM_LIMIT)


def small_cost(microseconds=0):
    return pl.CostEstimate(
        flops=1 + int(microseconds * 1e9),
        bytes_accessed=1 + int(microseconds * 3e6),
        transcendentals=0,
    )


class Fetches:
    def __init__(self, sems):
        self.sems = sems
        self.copies = []

    def add(self, source, target):
        self.copies.append(
            pltpu.make_async_copy(source, target, self.sems.at[len(self.copies)])
        )
        return len(self.copies) - 1

    def start(self):
        for copy in self.copies:
            copy.start()

    def wait(self, numbers):
        for number in numbers:
            self.copies[number].wait()


COPY, COLD = "copy", "cold"
SERVED_RANK, OWNED_RANK, COLD_GATE = 3, 4, 5


def hidden_kernel(blocks, slots, packing, width, *refs):
    hot_ref, refs = refs[0], refs[1:]
    row_refs, refs = refs[:blocks], refs[blocks:]
    up_ref, down_ref, copy_up_ref, copy_down_ref, pick_ref, base_ref, *refs = refs
    before_ref = refs.pop(0) if packing == 2 else None
    grad_ref, active_ref, *refs = refs
    part_ref = refs.pop(0) if COLD not in slots else None
    place_ref, packed_ref = (refs.pop(0), refs.pop(0)) if packing else (None, None)
    together, ups, downs, gates, slot_sems, block_sems = refs
    rows = row_refs[0].shape[0]
    hidden = down_ref.shape[1]
    group = 2 * rows

    def slot_copies(number, slot):
        index = 0 if slot == COPY else (1 - hot_ref[0] if slot == COLD else slot)
        up, down = (copy_up_ref, copy_down_ref) if slot == COPY else (up_ref, down_ref)
        return [
            pltpu.make_async_copy(up.at[index], ups.at[number], slot_sems.at[number, 0]),
            pltpu.make_async_copy(down.at[index], downs.at[number], slot_sems.at[number, 1]),
        ]

    block_copies = [
        pltpu.make_async_copy(ref, together.at[pl.ds(i * rows, rows)], block_sems.at[i])
        for i, ref in enumerate(row_refs)
    ]
    for copy in slot_copies(0, slots[0]) + block_copies:
        copy.start()
    for number in range(1, len(slots)):
        for copy in slot_copies(number, slots[number]):
            copy.start()
    first_gate = 0 if slots[0] == COPY else (COLD_GATE if slots[0] == COLD else 1)

    for number, slot in enumerate(slots):
        for copy in slot_copies(number, slot):
            copy.wait()
        to = pl.ds(number * hidden, hidden)

        for g in range(blocks // 2):
            here = slice(g * group, (g + 1) * group)
            if number == 0:
                for copy in block_copies[2 * g : 2 * g + 2]:
                    copy.wait()
                found = dot(pick_ref[...], together[here, 2 * width :], (1, 1))
                gates[:, here] = found
                if packing:
                    ranks = found[SERVED_RANK : OWNED_RANK + 1]
                    place = jnp.where(ranks > 0.5, base_ref[:, here] + ranks - 1.0, -1.0)
                    place_ref[:, here] = jnp.concatenate(
                        [place, jnp.zeros((6, group), F32)], axis=0
                    )
            gate = gates[first_gate + number : first_gate + number + 1, here]
            linear = dot(ups[number], together[here, :width], (0, 1))
            raw_grad = dot(downs[number], together[here, width : 2 * width], (1, 1))
            sigma = 0.5 * jnp.tanh(0.5 * linear) + 0.5
            active = (linear * sigma).astype(BF16).astype(F32)
            if part_ref is not None:
                part = jnp.sum(active * raw_grad, axis=0, keepdims=True)
                part_high, part_low = split_two(part)
                part_ref[pl.ds(16 * number, 16), here] = jnp.concatenate(
                    [part_high, part_low, jnp.zeros((14, group), BF16)], axis=0
                )
            active_ref[to, here] = (gate * active).astype(BF16)
            slope = sigma * (1.0 + linear * (1.0 - sigma))
            grad_ref[to, here] = (gate * raw_grad * slope).astype(BF16)

    if packing:
        moved_rows = packed_ref.shape[1]
        index = lax.broadcasted_iota(jnp.int32, (moved_rows, blocks * rows), 0)
        chosen = (index == place_ref[0:1, :].astype(jnp.int32)).astype(F32).astype(BF16)
        for half, ref in enumerate((grad_ref, active_ref)):
            to = slice(half * hidden, (half + 1) * hidden)
            found = dot(ref[:hidden, :], chosen, (1, 1))
            if before_ref is not None:
                found = found + before_ref[to, :].astype(F32)
            packed_ref[to, :] = found.astype(BF16)


def hidden_call(hot, blocks, weights, pick, base, slots, moved_rows=0, before=None):
    count = len(blocks)
    rows, columns = blocks[0].shape
    width, hidden = weights[0].shape[1:]
    total = count * rows
    packing = 0 if moved_rows == 0 else (1 if before is None else 2)
    vmem = pl.BlockSpec(memory_space=pltpu.VMEM)
    operands = [hot, *blocks, *weights, pick, base]
    in_specs = [pl.BlockSpec(memory_space=pltpu.SMEM)] + [ANYWHERE] * (count + 4) + [vmem] * 2
    if packing == 2:
        operands.append(before)
        in_specs.append(vmem)
    out_shape = [jax.ShapeDtypeStruct((len(slots) * hidden, total), BF16)] * 2
    if COLD not in slots:
        out_shape.append(jax.ShapeDtypeStruct((len(slots) * 16, total), BF16))
    if packing:
        out_shape.append(jax.ShapeDtypeStruct((8, total), F32))
        out_shape.append(jax.ShapeDtypeStruct((2 * hidden, moved_rows), BF16))
    return pl.pallas_call(
        functools.partial(hidden_kernel, count, slots, packing, width),
        in_specs=in_specs,
        out_specs=[vmem] * len(out_shape),
        out_shape=out_shape,
        scratch_shapes=[
            pltpu.VMEM((total, columns), BF16),
            pltpu.VMEM((len(slots), width, hidden), BF16),
            pltpu.VMEM((len(slots), hidden, width), BF16),
            pltpu.VMEM((16, total), F32),
            pltpu.SemaphoreType.DMA((len(slots), 2)),
            pltpu.SemaphoreType.DMA((count,)),
        ],
        compiler_params=call_params(),
        cost_estimate=small_cost(2 if COLD in slots else 0),
        name="hidden_units",
    )(*operands)


def fetch_pieces(fetches, pieces, expert, target):
    hidden = target.shape[0]
    found, column = [], 0
    for piece, first in pieces:
        count = piece.shape[1]
        source = piece
        if first is not None:
            start = pl.multiple_of((first + expert) * hidden, hidden)
            source = piece.at[pl.ds(start, hidden)]
        found.append(fetches.add(source, target.at[:, pl.ds(column, count)]))
        column += count
    return found


def chunk_copies_of(row_refs, tokens, cotan, width, sems):
    rows, chunk = row_refs[0].shape[0], tokens.shape[2]

    def copies(place, number, half):
        columns = pl.ds(pl.multiple_of(half * width + number * chunk, chunk), chunk)
        target = (tokens, cotan)[half]
        return [
            pltpu.make_async_copy(
                ref.at[:, columns],
                target.at[place, pl.ds(i * rows, rows)],
                sems.at[place, half, i],
            )
            for i, ref in enumerate(row_refs)
        ]

    return copies


def hot_kernel(blocks, firsts, width, *refs):
    hot_ref, refs = refs[0], refs[1:]
    row_refs, refs = refs[:blocks], refs[blocks:]
    pieces = len(firsts)
    grad_refs, active_refs, place_refs, refs = (
        refs[:pieces], refs[pieces : 2 * pieces], refs[2 * pieces : 3 * pieces], refs[3 * pieces :]
    )
    packed_ref, out_ref, grads, actives, tokens, cotan, sems, chunk_sems = refs
    chunks, total, chunk = tokens.shape
    hidden = grads.shape[0]
    fetches = Fetches(sems)
    of_rows = []
    for sources, target in ((grad_refs, grads), (active_refs, actives)):
        of_rows.append(fetch_pieces(fetches, list(zip(sources, firsts)), hot_ref[0], target))
    chunk_copies = chunk_copies_of(row_refs, tokens, cotan, width, chunk_sems)
    fetches.start()

    @pl.loop(0, chunks)
    def _(j):
        for copy in chunk_copies(j, j, 0) + chunk_copies(j, j, 1):
            copy.start()

    place = jnp.concatenate([ref[1:2, :] for ref in place_refs], axis=1)
    index = lax.broadcasted_iota(jnp.int32, (packed_ref.shape[1], total), 0)
    chosen = (index == place.astype(jnp.int32)).astype(F32).astype(BF16)
    for half, target in enumerate((grads, actives)):
        fetches.wait(of_rows[half])
        spread = dot(packed_ref[half * hidden : (half + 1) * hidden, :], chosen, (1, 0))
        target[...] = (target[...].astype(F32) + spread).astype(BF16)

    @pl.loop(0, chunks)
    def _(j):
        for half, (left, right) in enumerate(((grads, tokens), (actives, cotan))):
            for copy in chunk_copies(j, j, half):
                copy.wait()
            out_ref[j, half] = dot(left[...], right[j], (1, 0)).astype(BF16)


def hot_call(hot, blocks, firsts, grads, actives, places, packed, width, chunks):
    count = len(blocks)
    total = count * blocks[0].shape[0]
    chunk = width // chunks
    hidden = packed.shape[0] // 2
    vmem = pl.BlockSpec(memory_space=pltpu.VMEM)
    return pl.pallas_call(
        functools.partial(hot_kernel, count, firsts, width),
        in_specs=[pl.BlockSpec(memory_space=pltpu.SMEM)]
        + [ANYWHERE] * (count + 2 * len(firsts))
        + [vmem] * (len(firsts) + 1),
        out_specs=vmem,
        out_shape=jax.ShapeDtypeStruct((chunks, 2, hidden, chunk), BF16),
        scratch_shapes=[
            pltpu.VMEM((hidden, total), BF16),
            pltpu.VMEM((hidden, total), BF16),
            pltpu.VMEM((chunks, total, chunk), BF16),
            pltpu.VMEM((chunks, total, chunk), BF16),
            pltpu.SemaphoreType.DMA((2 * len(firsts),)),
            pltpu.SemaphoreType.DMA((chunks, 2, count)),
        ],
        compiler_params=call_params(),
        cost_estimate=small_cost(),
        name="hot_weight_grads",
    )(hot, *blocks, *grads, *actives, *places, packed)


def cold_kernel(blocks, firsts, width, *refs):
    hot_ref, chunk_ref, refs = refs[0], refs[1], refs[2:]
    row_refs, refs = refs[:blocks], refs[blocks:]
    pieces = len(firsts)
    grad_refs, active_refs, refs = refs[:pieces], refs[pieces : 2 * pieces], refs[2 * pieces :]
    near_ref, far_ref, grads, actives, tokens, cotan, sems, chunk_sems = refs
    fetches = Fetches(sems)
    of_rows = []
    for sources, target in ((grad_refs, grads), (active_refs, actives)):
        of_rows.append(fetch_pieces(fetches, list(zip(sources, firsts)), 1 - hot_ref[0], target))
    chunk_copies = chunk_copies_of(row_refs, tokens, cotan, width, chunk_sems)
    fetches.start()

    @pl.loop(0, 2)
    def _(j):
        for copy in chunk_copies(j, chunk_ref[j], 0) + chunk_copies(j, chunk_ref[j], 1):
            copy.start()

    for j, out_ref in enumerate((near_ref, far_ref)):
        for half, (left, right) in enumerate(((grads, tokens), (actives, cotan))):
            if j == 0:
                fetches.wait(of_rows[half])
            for copy in chunk_copies(j, chunk_ref[j], half):
                copy.wait()
            out_ref[half] = dot(left[...], right[j], (1, 0)).astype(BF16)


def cold_call(hot, chunk_pair, blocks, firsts, grads, actives, width, chunk):
    count = len(blocks)
    total = count * blocks[0].shape[0]
    hidden = grads[-1].shape[0]
    vmem = pl.BlockSpec(memory_space=pltpu.VMEM)
    smem = pl.BlockSpec(memory_space=pltpu.SMEM)
    return pl.pallas_call(
        functools.partial(cold_kernel, count, firsts, width),
        in_specs=[smem, smem] + [ANYWHERE] * (count + 2 * len(firsts)),
        out_specs=[vmem, vmem],
        out_shape=[jax.ShapeDtypeStruct((2, hidden, chunk), BF16)] * 2,
        scratch_shapes=[
            pltpu.VMEM((hidden, total), BF16),
            pltpu.VMEM((hidden, total), BF16),
            pltpu.VMEM((2, total, chunk), BF16),
            pltpu.VMEM((2, total, chunk), BF16),
            pltpu.SemaphoreType.DMA((2 * len(firsts),)),
            pltpu.SemaphoreType.DMA((2, 2, count)),
        ],
        compiler_params=call_params(),
        cost_estimate=small_cost(2),
        name="cold_weight_grads",
    )(hot, chunk_pair, *blocks, *grads, *actives)


def place_kernel(flags_ref, hot_ref, moved_ref, kept_ref, across_ref, up_ref, down_ref):
    hot_slot = flags_ref[0]
    up_ref[hot_slot] = hot_ref[0].T
    down_ref[hot_slot] = hot_ref[1]

    def place_cold(other_ref):
        up = (moved_ref[0].astype(F32) + other_ref[0].astype(F32)).astype(BF16)
        up_ref[1 - hot_slot] = up.T
        down = (moved_ref[1].astype(F32) + other_ref[1].astype(F32)).astype(BF16)
        down_ref[1 - hot_slot] = down

    at_end = flags_ref[1] == 1
    pl.when(at_end)(lambda: place_cold(kept_ref))
    pl.when(jnp.logical_not(at_end))(lambda: place_cold(across_ref))


def place_call(flags, hot_sum, moved, kept, across):
    hidden, chunk = hot_sum.shape[1:]
    vmem = pl.BlockSpec(memory_space=pltpu.VMEM)
    return pl.pallas_call(
        place_kernel,
        in_specs=[pl.BlockSpec(memory_space=pltpu.SMEM)] + [vmem] * 4,
        out_specs=[vmem, vmem],
        out_shape=[
            jax.ShapeDtypeStruct((2, chunk, hidden), BF16),
            jax.ShapeDtypeStruct((2, hidden, chunk), BF16),
        ],
        compiler_params=call_params(),
        cost_estimate=small_cost(),
        name="place_weight_grads",
    )(flags, hot_sum, moved, kept, across)


class RowSums:
    def __init__(self, half, lefts, own, copied, outs, scratch, parts=None, pick=None, arrived=None):
        self.half, self.own, self.copied, self.outs = half, own, copied, outs
        self.parts, self.pick, self.arrived_ref = parts, pick, arrived
        self.is_output = parts is not None
        self.left, self.weights, self.out, *rest = scratch
        self.arrived = rest.pop(0) if arrived is not None else None
        left_sems, self.chunk_sems, self.out_sems = rest
        self.hidden, self.width = own.shape[1:] if self.is_output else own.shape[:0:-1]
        self.step = self.weights.shape[3] if self.is_output else self.weights.shape[2]
        self.chunks, self.slots = self.weights.shape[:2]
        self.tail = pl.ds(self.width, self.out.shape[1] - self.width)
        self.of_left = Fetches(left_sems)
        row, column = 0, 0
        for ref in lefts:
            count = ref.shape[1] // 2
            self.of_left.add(
                ref.at[:, pl.ds(half * count, count)],
                self.left.at[pl.ds(row, ref.shape[0]), pl.ds(column, count)],
            )
            row += ref.shape[0]
            if row == self.left.shape[0]:
                row, column = 0, column + count

    def columns(self, j):
        return pl.ds(pl.multiple_of(j * self.step, self.step), self.step)

    def chunk_copies(self, j):
        here = self.columns(j)
        found = []
        for slot in range(self.slots):
            source = self.copied.at[0] if slot == 0 else self.own.at[slot - 1]
            source = source.at[:, here] if self.is_output else source.at[here]
            found.append(
                pltpu.make_async_copy(
                    source, self.weights.at[j, slot], self.chunk_sems.at[j, slot]
                )
            )
        if self.arrived is not None:
            found.append(
                pltpu.make_async_copy(
                    self.arrived_ref.at[:, here],
                    self.arrived.at[:, here],
                    self.chunk_sems.at[j, self.slots],
                )
            )
        return found

    def tail_copies(self):
        if self.arrived is None or not self.is_output:
            return []
        return [
            pltpu.make_async_copy(
                self.arrived_ref.at[:, self.tail],
                self.arrived.at[:, self.tail],
                self.chunk_sems.at[self.chunks, 0],
            )
        ]

    def stores(self, here, number):
        rows = self.out.shape[0] // len(self.outs)
        return [
            pltpu.make_async_copy(
                self.out.at[pl.ds(i * rows, rows), here],
                ref.at[:, here],
                self.out_sems.at[number, i],
            )
            for i, ref in enumerate(self.outs)
        ]

    def store(self, here, number, values):
        if self.arrived is not None:
            values = values + self.arrived[:, here].astype(F32)
        self.out[:, here] = values.astype(BF16)
        for copy in self.stores(here, number):
            copy.start()

    def start(self):
        self.of_left.start()

        @pl.loop(0, self.chunks)
        def _(j):
            for copy in self.chunk_copies(j):
                copy.start()

        for copy in self.tail_copies():
            copy.start()

    def compute(self):
        self.of_left.wait(range(len(self.of_left.copies)))

        @pl.loop(0, self.chunks)
        def _(j):
            for copy in self.chunk_copies(j):
                copy.wait()
            if self.is_output:
                right = self.weights[j].reshape(self.slots * self.hidden, self.step)
                values = dot(self.left[...], right, (0, 0))
            else:
                right = jnp.concatenate(
                    [self.weights[j, slot] for slot in range(self.slots)], axis=1
                )
                values = dot(self.left[...], right, (0, 1))
            self.store(self.columns(j), j, values)

        if self.is_output:
            tables, stacked = [], []
            for ref in self.parts:
                count = ref.shape[1] // 2
                stacked.append(ref[:, self.half * count : (self.half + 1) * count])
                if sum(values.shape[0] for values in stacked) == self.pick.shape[0]:
                    tables.append(jnp.concatenate(stacked, axis=0))
                    stacked = []
            table = jnp.concatenate(tables, axis=1)
            for copy in self.tail_copies():
                copy.wait()
            self.store(self.tail, self.chunks, dot(table, self.pick[...], (0, 0)))

    def finish(self):
        @pl.loop(0, self.chunks)
        def _(j):
            for copy in self.stores(self.columns(j), j):
                copy.wait()

        if self.is_output:
            for copy in self.stores(self.tail, self.chunks):
                copy.wait()


def rows_kernel(half, pieces, with_arrived, *refs):
    def take(count):
        nonlocal refs
        found, refs = refs[:count], refs[count:]
        return found

    grads, actives, parts = take(pieces), take(pieces), take(pieces)
    up, copy_up, down, copy_down, pick = take(5)
    arrived = take(2) if with_arrived else (None, None)
    outs = 4 if with_arrived else 1
    gradient_outs, output_outs = take(outs), take(outs)
    scratch = 7 if with_arrived else 6
    gradient = RowSums(
        half, grads, up, copy_up, gradient_outs, take(scratch), arrived=arrived[0]
    )
    output = RowSums(
        half, actives, down, copy_down, output_outs, take(scratch), parts, pick, arrived[1]
    )
    for part in (gradient, output):
        part.start()
    for part in (gradient, output):
        part.compute()
    for part in (gradient, output):
        part.finish()


def rows_call(half, grads, actives, parts, weights, pick, arrived=()):
    own_up, own_down, copy_up, copy_down = weights
    slots = own_up.shape[0] + 1
    width, hidden = own_up.shape[1:]
    total = sum(a.shape[1] * a.shape[0] for a in grads) // (2 * slots * hidden)
    step = 512
    chunks = width // step
    outs = 4 if arrived else 1
    vmem = pl.BlockSpec(memory_space=pltpu.VMEM)
    operands = [*grads, *actives, *parts, own_up, copy_up, own_down, copy_down, pick, *arrived]
    in_specs = (
        [ANYWHERE] * (2 * len(grads))
        + [vmem] * len(parts)
        + [ANYWHERE] * 4
        + [vmem]
        + [ANYWHERE] * len(arrived)
    )
    out_shape, scratch = [], []
    for columns, tile in (
        (width, (step, hidden)),
        (width + pick.shape[1], (hidden, step)),
    ):
        out_shape += [jax.ShapeDtypeStruct((total // outs, columns), BF16)] * outs
        scratch += [
            pltpu.VMEM((slots * hidden, total), BF16),
            pltpu.VMEM((chunks, slots) + tile, BF16),
            pltpu.VMEM((total, columns), BF16),
        ]
        if arrived:
            scratch.append(pltpu.VMEM((total, columns), BF16))
        scratch += [
            pltpu.SemaphoreType.DMA((len(grads),)),
            pltpu.SemaphoreType.DMA((chunks + 1, slots + 1)),
            pltpu.SemaphoreType.DMA((chunks + 1, outs)),
        ]
    return pl.pallas_call(
        functools.partial(rows_kernel, half, len(grads), bool(arrived)),
        in_specs=in_specs,
        out_specs=[ANYWHERE] * len(out_shape),
        out_shape=out_shape,
        scratch_shapes=scratch,
        compiler_params=call_params(),
        cost_estimate=small_cost(),
        name="row_sums",
    )(*operands)


class CubeExchange:
    def __init__(self):
        self.first = [(i, i ^ (4 if i & 1 else 2)) for i in range(8)]
        self.second = [(i, i ^ (2 if i & 1 else 4)) for i in range(8)]
        self.mate = [(i, i ^ 1) for i in range(8)]

    def sources(self, me):
        first = jnp.where(me % 2 == 1, 4, 2)
        second = 6 - first
        zero = jnp.zeros_like(me)
        return me ^ jnp.stack(
            [zero, zero + 1, first, second, second + 1, first + 1, zero + 6, zero + 7]
        )

    def first_hop(self, block):
        return lax.ppermute(block, "expert", self.first)

    def far(self, first_block):
        return lax.ppermute(first_block, "expert", self.second)

    def to_mate(self, block):
        return lax.ppermute(block, "expert", self.mate)

    def reduce(self, blocks):
        own, a, b, d = blocks
        d_arrived = lax.ppermute(d, "expert", self.second)
        b_arrived = lax.ppermute(b, "expert", self.second)
        a = (a.astype(F32) + d_arrived.astype(F32)).astype(BF16)
        a_arrived = lax.ppermute(a, "expert", self.first)
        return own.astype(F32) + a_arrived.astype(F32) + b_arrived.astype(F32)


class PlainExchange:
    def __init__(self, count):
        self.count = count

    def sources(self, me):
        return jnp.arange(self.count, dtype=jnp.int32)

    def gather(self, block):
        return lax.all_gather(block, "expert", tiled=True)

    def reduce(self, partial):
        return lax.psum_scatter(
            partial.astype(BF16), "expert", scatter_dimension=0, tiled=True
        ).astype(F32)


def local(
    tokens,
    cotangent,
    gate_weights,
    expert_ids,
    copy_pick,
    copy_expert,
    up_weight,
    down_weight,
    copy_up,
    copy_down,
):
    device_count = lax.axis_size("expert")
    me = lax.axis_index("expert")
    rows, width = tokens.shape
    chosen = expert_ids.shape[1]
    local_count = up_weight.shape[0]
    hidden = up_weight.shape[2]
    expert_count = local_count * device_count
    moved_most = 3 * (rows * chosen // expert_count) // 8
    moved_rows = padded(device_count * moved_most, 128)

    column_count = expert_count + device_count
    owner = expert_ids // local_count
    column = jnp.where(copy_pick == 1, expert_count + owner, expert_ids)
    hit = column[:, :, None] == jnp.arange(column_count, dtype=jnp.int32)
    gates = jnp.sum(jnp.where(hit, gate_weights[:, :, None], 0.0), axis=1)
    moved = jnp.sum(hit[:, :, expert_count:].astype(F32), axis=1)
    lower = (
        jnp.arange(rows, dtype=jnp.int32)[:, None] >= jnp.arange(rows, dtype=jnp.int32)[None, :]
    )
    rank = dot(lower.astype(BF16), moved.astype(BF16), (1, 0)) * moved
    gate_high, gate_low = split_two(gates)
    table_width = padded(2 * column_count + device_count, 128)
    table = jnp.concatenate(
        [
            gate_high,
            gate_low,
            rank.astype(BF16),
            jnp.zeros((rows, table_width - 2 * column_count - device_count), BF16),
        ],
        axis=1,
    )
    behind = (me + device_count - 1) % device_count
    columns = [local_count * me + i for i in range(local_count)] + [expert_count + behind]
    slots = len(columns)
    table_rows = jnp.arange(table_width, dtype=jnp.int32)
    wanted = jnp.stack(columns)
    high_pick = (table_rows[:, None] == wanted[None, :]).astype(BF16)
    low_pick = (table_rows[:, None] == wanted[None, :] + column_count).astype(BF16)
    wanted_rank = 2 * column_count + jnp.stack([behind, me])
    rank_pick = (table_rows[:, None] == wanted_rank[None, :]).astype(BF16)
    to_owner = [(i, (i - 1) % device_count) for i in range(device_count)]
    hot_slot = copy_expert[(me + 1) % device_count] % local_count
    own_width = local_count * hidden

    def finish(output_sum, gradient_sum, table_sum):
        grads = table_sum[:, :column_count] + table_sum[:, column_count : 2 * column_count]
        gate_grad = jnp.sum(jnp.where(hit, grads[:, None, :], 0.0), axis=2)
        return output_sum.astype(BF16), gradient_sum.astype(BF16), gate_grad

    replicas = lax.axis_size("dp")
    if device_count == 8 and local_count == 2 and replicas == 4:
        exchange = CubeExchange()
        replica = lax.axis_index("dp")
        hot = hot_slot.reshape(1).astype(jnp.int32)
        cold_column = local_count * me + 1 - hot_slot
        weights = (up_weight, down_weight, copy_up, copy_down)
        base = jnp.repeat((exchange.sources(me) * moved_most).astype(F32), rows)[None, :]
        slot_columns = jnp.stack([wanted[slots - 1], wanted[0], wanted[1]])
        pick_columns = jnp.stack(
            [wanted[slots - 1], wanted[0], wanted[1], wanted_rank[0], wanted_rank[1], cold_column]
            + [jnp.int32(-1)] * 10
        )
        is_gate = jnp.array([1, 1, 1, 0, 0, 1] + [0] * 10, jnp.int32)
        pick = (
            (table_rows[None, :] == pick_columns[:, None])
            | (
                (table_rows[None, :] == pick_columns[:, None] + column_count)
                & (is_gate[:, None] == 1)
            )
        ).astype(BF16)
        part_columns = jnp.stack(
            [slot_columns, slot_columns + column_count] + [jnp.full((slots,), -1, jnp.int32)] * 14,
            axis=1,
        ).reshape(-1)
        part_pick = (table_rows[None, :] == part_columns[:, None]).astype(BF16)

        own = jnp.concatenate([tokens, cotangent, table], axis=1)
        own_mate = exchange.to_mate(own)
        a, b = exchange.first_hop(own), exchange.far(own)
        replica_pairs = [(0, 1), (1, 0), (2, 3), (3, 2)]
        other = lax.ppermute(own, "dp", replica_pairs)
        blocks_1 = [own, own_mate]
        ends = (2 * rows, 6 * rows)
        grad_1, active_1, part_1, place_1, packed = hidden_call(
            hot, blocks_1, weights, pick, base[:, : ends[0]], (COPY, 0, 1), moved_rows
        )
        a, b, grad_1 = lax.optimization_barrier((a, b, grad_1))
        d = exchange.far(a)
        a_mate = exchange.to_mate(a)
        other, a_mate = lax.optimization_barrier((other, a_mate))
        blocks_2 = [a, b, a_mate, exchange.to_mate(b)]
        grad_2, active_2, part_2, place_2, packed = hidden_call(
            hot, blocks_2, weights, pick, base[:, ends[0] : ends[1]], (COPY, 0, 1), moved_rows,
            packed,
        )
        grad_2, d = lax.optimization_barrier((grad_2, d))
        blocks_3 = [d, exchange.to_mate(d)]
        blocks = blocks_1 + blocks_2 + blocks_3

        other_a = exchange.first_hop(other)

        late_base = base[:, ends[1] :]
        grad_copy, active_copy, part_copy, place_3, packed = hidden_call(
            hot, blocks_3, weights, pick, late_base, (COPY,), moved_rows, packed
        )
        packed = lax.ppermute(packed, "expert", to_owner)
        grad_3, active_3, part_3 = hidden_call(hot, blocks_3, weights, pick, late_base, (0, 1))
        packed, grad_3, other, other_a = lax.optimization_barrier(
            (packed, grad_3, other, other_a)
        )
        other_b = exchange.far(other)
        other_d = exchange.far(other_a)
        hot_grads = hot_call(
            hot, blocks, (1, 1, 0), (grad_1, grad_2, grad_3), (active_1, active_2, active_3),
            (place_1, place_2, place_3), packed, width, replicas,
        )
        hot_sum = lax.psum_scatter(hot_grads, "dp", scatter_dimension=0, tiled=True)[0]

        grad_3, active_3, other_b, _ = lax.optimization_barrier(
            (grad_3, active_3, other_b, hot_grads)
        )
        sides = (
            (grad_1, grad_2, grad_copy, grad_3),
            (active_1, active_2, active_copy, active_3),
            (part_1, part_2, part_copy, part_3),
            weights, part_pick,
        )
        mates_rows = rows_call(1, *sides)
        arrived = [exchange.to_mate(block) for block in mates_rows]
        other_d, _ = lax.optimization_barrier((other_d, mates_rows[0]))
        pair_blocks = [other, other_a, other_b, other_d]
        pair_blocks = pair_blocks + [exchange.to_mate(block) for block in pair_blocks]
        *pair_blocks, _ = lax.optimization_barrier((*pair_blocks, mates_rows[0]))
        grad_pair, active_pair = hidden_call(hot, pair_blocks, weights, pick, base, (COLD,))
        chunk_pairs = jnp.array([[1, 0], [3, 2], [0, 1], [2, 3]], jnp.int32)
        given, second = cold_call(
            hot, chunk_pairs[replica], blocks + pair_blocks, (1, 1, 0, None),
            (grad_1, grad_2, grad_3, grad_pair), (active_1, active_2, active_3, active_pair),
            width, width // replicas,
        )
        *arrived, _ = lax.optimization_barrier((*arrived, given))
        own_rows = rows_call(0, *sides, tuple(arrived))
        gradient_rows, output_rows = own_rows[:4], own_rows[4:]
        gradient_sum = exchange.reduce(gradient_rows)
        output_sum = exchange.reduce(output_rows)
        moved = lax.ppermute(given, "dp", [(0, 1), (1, 3), (2, 0), (3, 2)])
        moved, to_middle = lax.optimization_barrier((moved, second))
        across = lax.ppermute(to_middle, "dp", [(1, 2), (2, 1)])
        at_end = (replica == 0) | (replica == replicas - 1)
        up_grad, down_grad = place_call(
            jnp.stack([hot_slot, at_end.astype(jnp.int32)]).astype(jnp.int32),
            hot_sum, moved, second, across,
        )
        return (*finish(output_sum[:, :width], gradient_sum, output_sum[:, width:]), up_grad, down_grad)

    exchange = PlainExchange(device_count)
    up_all = jnp.concatenate([up_weight[i] for i in range(local_count)] + [copy_up[0]], axis=1)
    down_all = jnp.concatenate(
        [down_weight[i] for i in range(local_count)] + [copy_down[0]], axis=0
    )

    def some_rows(own_block):
        gathered = exchange.gather(own_block)
        all_tokens = gathered[:, :width]
        all_cotangent = gathered[:, width : 2 * width]
        all_table = gathered[:, 2 * width :]
        slot_gates = dot(all_table, high_pick + low_pick, (1, 0))
        ranks = dot(all_table, rank_pick, (1, 0)).astype(jnp.int32)
        base = jnp.repeat(exchange.sources(me) * moved_most, own_block.shape[0])
        place = jnp.where(ranks > 0, base[:, None] + ranks - 1, -1)
        moved_index = jnp.arange(moved_rows, dtype=jnp.int32)[None, :]
        served_place = (place[:, :1] == moved_index).astype(BF16)
        owned_place = (place[:, 1:] == moved_index).astype(BF16)
        linear = dot(all_tokens, up_all, (1, 0))
        raw_grad = dot(all_cotangent, down_all, (1, 1))
        spread = jnp.repeat(slot_gates, hidden, axis=1)
        sigma = jax.nn.sigmoid(linear)
        active = (linear * sigma).astype(BF16).astype(F32)
        gate_part = jnp.sum((active * raw_grad).reshape(-1, slots, hidden), axis=2)
        weighted = (spread * active).astype(BF16)
        slope = sigma * (1.0 + linear * (1.0 - sigma))
        linear_grad = (spread * raw_grad * slope).astype(BF16)
        both = jnp.concatenate([linear_grad[:, own_width:], weighted[:, own_width:]], axis=1)
        packed = dot(served_place, both, (0, 0)).astype(BF16)
        packed = lax.ppermute(packed, "expert", to_owner)
        unpacked = dot(owned_place, packed, (1, 0)).astype(BF16)
        up_parts = []
        down_parts = []
        for i in range(local_count):
            here = (hot_slot == i).astype(BF16)
            part = slice(i * hidden, (i + 1) * hidden)
            total_grad = linear_grad[:, part] + unpacked[:, :hidden] * here
            total_active = weighted[:, part] + unpacked[:, hidden:] * here
            up_parts.append(dot(all_tokens, total_grad, (0, 0)))
            down_parts.append(dot(total_active, all_cotangent, (0, 0)))
        mixed = dot(weighted, down_all, (1, 0)).astype(BF16)
        back = dot(linear_grad, up_all, (1, 1)).astype(BF16)
        part_high, part_low = split_two(gate_part)
        grad_table = dot(part_high, high_pick, (1, 1)) + dot(part_low, low_pick, (1, 1))
        summed = exchange.reduce(
            jnp.concatenate([mixed, back, grad_table.astype(BF16)], axis=1)
        )
        return summed, jnp.stack(up_parts), jnp.stack(down_parts)

    own = jnp.concatenate([tokens, cotangent, table], axis=1)
    pieces = max(1, device_count // 8)
    if pieces == 1:
        summed, up_sum, down_sum = some_rows(own)
    else:

        def step(totals, piece):
            summed, up_part, down_part = some_rows(piece)
            return (totals[0] + up_part, totals[1] + down_part), summed

        zeros = (jnp.zeros(up_weight.shape, F32), jnp.zeros(down_weight.shape, F32))
        (up_sum, down_sum), summed = lax.scan(
            step, zeros, own.reshape(pieces, rows // pieces, own.shape[1])
        )
        summed = summed.reshape(rows, own.shape[1])
    up_grad = lax.psum_scatter(up_sum.astype(BF16), "dp", scatter_dimension=1, tiled=True)
    down_grad = lax.psum_scatter(down_sum.astype(BF16), "dp", scatter_dimension=2, tiled=True)
    parts = (summed[:, :width], summed[:, width : 2 * width], summed[:, 2 * width :])
    return (*finish(*parts), up_grad, down_grad)


def solution(mesh):
    placed = (
        P(("expert", "dp"), None),
        P(("expert", "dp"), None),
        P(("expert", "dp"), None),
        P(("expert", "dp"), None),
        P(("expert", "dp"), None),
        P(),
        P("expert", None, None),
        P("expert", None, None),
        P("expert", None, None),
        P("expert", None, None),
    )
    return jax.shard_map(
        local,
        mesh=mesh,
        in_specs=placed,
        out_specs=(
            P(("expert", "dp"), None),
            P(("expert", "dp"), None),
            P(("expert", "dp"), None),
            P("expert", "dp", None),
            P("expert", None, "dp"),
        ),
        check_vma=False,
    )
```

```python
import functools

import jax
import jax.numpy as jnp
from jax import lax
from jax.experimental import pallas as pl
from jax.experimental.pallas import tpu as pltpu
from jax.sharding import PartitionSpec as P

BF16 = jnp.bfloat16
F32 = jnp.float32


def padded(count, multiple):
    return -(-count // multiple) * multiple


def dot(a, b, contract):
    return lax.dot_general(a, b, ((contract[:1], contract[1:]), ((), ())), preferred_element_type=F32)


def split_two(values):
    high = values.astype(BF16)
    return high, (values - high.astype(F32)).astype(BF16)


VMEM_LIMIT = 64 * 1024 * 1024
ANYWHERE = pl.BlockSpec(memory_space=pl.ANY)


def call_params():
    return pltpu.CompilerParams(vmem_limit_bytes=VMEM_LIMIT)


def small_cost(microseconds=0):
    return pl.CostEstimate(
        flops=1 + int(microseconds * 1e9),
        bytes_accessed=1 + int(microseconds * 3e6),
        transcendentals=0,
    )


class Fetches:
    def __init__(self, sems):
        self.sems = sems
        self.copies = []

    def add(self, source, target):
        self.copies.append(
            pltpu.make_async_copy(source, target, self.sems.at[len(self.copies)])
        )
        return len(self.copies) - 1

    def start(self):
        for copy in self.copies:
            copy.start()

    def wait(self, numbers):
        for number in numbers:
            self.copies[number].wait()


COPY, COLD = "copy", "cold"
SERVED_RANK, OWNED_RANK, COLD_GATE = 3, 4, 5


def hidden_kernel(blocks, slots, packing, width, *refs):
    hot_ref, refs = refs[0], refs[1:]
    row_refs, refs = refs[:blocks], refs[blocks:]
    up_ref, down_ref, copy_up_ref, copy_down_ref, pick_ref, base_ref, *refs = refs
    before_ref = refs.pop(0) if packing == 2 else None
    grad_ref, active_ref, *refs = refs
    part_ref = refs.pop(0) if COLD not in slots else None
    place_ref, packed_ref = (refs.pop(0), refs.pop(0)) if packing else (None, None)
    together, ups, downs, gates, slot_sems, block_sems = refs
    rows = row_refs[0].shape[0]
    hidden = down_ref.shape[1]
    group = 2 * rows

    def slot_copies(number, slot):
        index = 0 if slot == COPY else (1 - hot_ref[0] if slot == COLD else slot)
        up, down = (copy_up_ref, copy_down_ref) if slot == COPY else (up_ref, down_ref)
        return [
            pltpu.make_async_copy(up.at[index], ups.at[number], slot_sems.at[number, 0]),
            pltpu.make_async_copy(down.at[index], downs.at[number], slot_sems.at[number, 1]),
        ]

    block_copies = [
        pltpu.make_async_copy(ref, together.at[pl.ds(i * rows, rows)], block_sems.at[i])
        for i, ref in enumerate(row_refs)
    ]
    for copy in slot_copies(0, slots[0]) + block_copies:
        copy.start()
    for number in range(1, len(slots)):
        for copy in slot_copies(number, slots[number]):
            copy.start()
    first_gate = 0 if slots[0] == COPY else (COLD_GATE if slots[0] == COLD else 1)

    for number, slot in enumerate(slots):
        for copy in slot_copies(number, slot):
            copy.wait()
        to = pl.ds(number * hidden, hidden)

        for g in range(blocks // 2):
            here = slice(g * group, (g + 1) * group)
            if number == 0:
                for copy in block_copies[2 * g : 2 * g + 2]:
                    copy.wait()
                found = dot(pick_ref[...], together[here, 2 * width :], (1, 1))
                gates[:, here] = found
                if packing:
                    ranks = found[SERVED_RANK : OWNED_RANK + 1]
                    place = jnp.where(ranks > 0.5, base_ref[:, here] + ranks - 1.0, -1.0)
                    place_ref[:, here] = jnp.concatenate(
                        [place, jnp.zeros((6, group), F32)], axis=0
                    )
            gate = gates[first_gate + number : first_gate + number + 1, here]
            linear = dot(ups[number], together[here, :width], (0, 1))
            raw_grad = dot(downs[number], together[here, width : 2 * width], (1, 1))
            sigma = 0.5 * jnp.tanh(0.5 * linear) + 0.5
            active = (linear * sigma).astype(BF16).astype(F32)
            if part_ref is not None:
                part = jnp.sum(active * raw_grad, axis=0, keepdims=True)
                part_high, part_low = split_two(part)
                part_ref[pl.ds(16 * number, 16), here] = jnp.concatenate(
                    [part_high, part_low, jnp.zeros((14, group), BF16)], axis=0
                )
            active_ref[to, here] = (gate * active).astype(BF16)
            slope = sigma * (1.0 + linear * (1.0 - sigma))
            grad_ref[to, here] = (gate * raw_grad * slope).astype(BF16)

    if packing:
        moved_rows = packed_ref.shape[1]
        index = lax.broadcasted_iota(jnp.int32, (moved_rows, blocks * rows), 0)
        chosen = (index == place_ref[0:1, :].astype(jnp.int32)).astype(F32).astype(BF16)
        for half, ref in enumerate((grad_ref, active_ref)):
            to = slice(half * hidden, (half + 1) * hidden)
            found = dot(ref[:hidden, :], chosen, (1, 1))
            if before_ref is not None:
                found = found + before_ref[to, :].astype(F32)
            packed_ref[to, :] = found.astype(BF16)


def hidden_call(hot, blocks, weights, pick, base, slots, moved_rows=0, before=None):
    count = len(blocks)
    rows, columns = blocks[0].shape
    width, hidden = weights[0].shape[1:]
    total = count * rows
    packing = 0 if moved_rows == 0 else (1 if before is None else 2)
    vmem = pl.BlockSpec(memory_space=pltpu.VMEM)
    operands = [hot, *blocks, *weights, pick, base]
    in_specs = [pl.BlockSpec(memory_space=pltpu.SMEM)] + [ANYWHERE] * (count + 4) + [vmem] * 2
    if packing == 2:
        operands.append(before)
        in_specs.append(vmem)
    out_shape = [jax.ShapeDtypeStruct((len(slots) * hidden, total), BF16)] * 2
    if COLD not in slots:
        out_shape.append(jax.ShapeDtypeStruct((len(slots) * 16, total), BF16))
    if packing:
        out_shape.append(jax.ShapeDtypeStruct((8, total), F32))
        out_shape.append(jax.ShapeDtypeStruct((2 * hidden, moved_rows), BF16))
    return pl.pallas_call(
        functools.partial(hidden_kernel, count, slots, packing, width),
        in_specs=in_specs,
        out_specs=[vmem] * len(out_shape),
        out_shape=out_shape,
        scratch_shapes=[
            pltpu.VMEM((total, columns), BF16),
            pltpu.VMEM((len(slots), width, hidden), BF16),
            pltpu.VMEM((len(slots), hidden, width), BF16),
            pltpu.VMEM((16, total), F32),
            pltpu.SemaphoreType.DMA((len(slots), 2)),
            pltpu.SemaphoreType.DMA((count,)),
        ],
        compiler_params=call_params(),
        cost_estimate=small_cost(2 if COLD in slots else 0),
        name="hidden_units",
    )(*operands)


def fetch_pieces(fetches, pieces, expert, target):
    hidden = target.shape[0]
    found, column = [], 0
    for piece, first in pieces:
        count = piece.shape[1]
        source = piece
        if first is not None:
            start = pl.multiple_of((first + expert) * hidden, hidden)
            source = piece.at[pl.ds(start, hidden)]
        found.append(fetches.add(source, target.at[:, pl.ds(column, count)]))
        column += count
    return found


def chunk_copies_of(row_refs, tokens, cotan, width, sems):
    rows, chunk = row_refs[0].shape[0], tokens.shape[2]

    def copies(place, number, half):
        columns = pl.ds(pl.multiple_of(half * width + number * chunk, chunk), chunk)
        target = (tokens, cotan)[half]
        return [
            pltpu.make_async_copy(
                ref.at[:, columns],
                target.at[place, pl.ds(i * rows, rows)],
                sems.at[place, half, i],
            )
            for i, ref in enumerate(row_refs)
        ]

    return copies


def hot_kernel(blocks, firsts, width, *refs):
    hot_ref, refs = refs[0], refs[1:]
    row_refs, refs = refs[:blocks], refs[blocks:]
    pieces = len(firsts)
    grad_refs, active_refs, place_refs, refs = (
        refs[:pieces], refs[pieces : 2 * pieces], refs[2 * pieces : 3 * pieces], refs[3 * pieces :]
    )
    packed_ref, out_ref, grads, actives, tokens, cotan, out, sems, chunk_sems, out_sems = refs
    chunks, total, chunk = tokens.shape
    hidden = grads.shape[0]
    fetches = Fetches(sems)
    of_rows = []
    for sources, target in ((grad_refs, grads), (active_refs, actives)):
        of_rows.append(fetch_pieces(fetches, list(zip(sources, firsts)), hot_ref[0], target))
    chunk_copies = chunk_copies_of(row_refs, tokens, cotan, width, chunk_sems)
    fetches.start()

    @pl.loop(0, chunks)
    def _(j):
        for copy in chunk_copies(j, j, 0) + chunk_copies(j, j, 1):
            copy.start()

    def store_of(j):
        return pltpu.make_async_copy(out.at[j], out_ref.at[j], out_sems.at[j])

    place = jnp.concatenate([ref[1:2, :] for ref in place_refs], axis=1)
    index = lax.broadcasted_iota(jnp.int32, (packed_ref.shape[1], total), 0)
    chosen = (index == place.astype(jnp.int32)).astype(F32).astype(BF16)
    for half, target in enumerate((grads, actives)):
        fetches.wait(of_rows[half])
        spread = dot(packed_ref[half * hidden : (half + 1) * hidden, :], chosen, (1, 0))
        target[...] = (target[...].astype(F32) + spread).astype(BF16)

    @pl.loop(0, chunks)
    def _(j):
        for half, (left, right) in enumerate(((grads, tokens), (actives, cotan))):
            for copy in chunk_copies(j, j, half):
                copy.wait()
            out[j, half] = dot(left[...], right[j], (1, 0)).astype(BF16)
        store_of(j).start()

    @pl.loop(0, chunks)
    def _(j):
        store_of(j).wait()


def hot_call(hot, blocks, firsts, grads, actives, places, packed, width, chunks):
    count = len(blocks)
    total = count * blocks[0].shape[0]
    chunk = width // chunks
    hidden = packed.shape[0] // 2
    vmem = pl.BlockSpec(memory_space=pltpu.VMEM)
    return pl.pallas_call(
        functools.partial(hot_kernel, count, firsts, width),
        in_specs=[pl.BlockSpec(memory_space=pltpu.SMEM)]
        + [ANYWHERE] * (count + 2 * len(firsts))
        + [vmem] * (len(firsts) + 1),
        out_specs=ANYWHERE,
        out_shape=jax.ShapeDtypeStruct((chunks, 2, hidden, chunk), BF16),
        scratch_shapes=[
            pltpu.VMEM((hidden, total), BF16),
            pltpu.VMEM((hidden, total), BF16),
            pltpu.VMEM((chunks, total, chunk), BF16),
            pltpu.VMEM((chunks, total, chunk), BF16),
            pltpu.VMEM((chunks, 2, hidden, chunk), BF16),
            pltpu.SemaphoreType.DMA((2 * len(firsts),)),
            pltpu.SemaphoreType.DMA((chunks, 2, count)),
            pltpu.SemaphoreType.DMA((chunks,)),
        ],
        compiler_params=call_params(),
        cost_estimate=small_cost(),
        name="hot_weight_grads",
    )(hot, *blocks, *grads, *actives, *places, packed)


def cold_kernel(blocks, firsts, width, *refs):
    hot_ref, chunk_ref, refs = refs[0], refs[1], refs[2:]
    row_refs, refs = refs[:blocks], refs[blocks:]
    pieces = len(firsts)
    grad_refs, active_refs, refs = refs[:pieces], refs[pieces : 2 * pieces], refs[2 * pieces :]
    near_ref, far_ref, grads, actives, tokens, cotan, sems, chunk_sems = refs
    fetches = Fetches(sems)
    of_rows = []
    for sources, target in ((grad_refs, grads), (active_refs, actives)):
        of_rows.append(fetch_pieces(fetches, list(zip(sources, firsts)), 1 - hot_ref[0], target))
    chunk_copies = chunk_copies_of(row_refs, tokens, cotan, width, chunk_sems)
    fetches.start()

    @pl.loop(0, 2)
    def _(j):
        for copy in chunk_copies(j, chunk_ref[j], 0) + chunk_copies(j, chunk_ref[j], 1):
            copy.start()

    for j, out_ref in enumerate((near_ref, far_ref)):
        for half, (left, right) in enumerate(((grads, tokens), (actives, cotan))):
            if j == 0:
                fetches.wait(of_rows[half])
            for copy in chunk_copies(j, chunk_ref[j], half):
                copy.wait()
            out_ref[half] = dot(left[...], right[j], (1, 0)).astype(BF16)


def cold_call(hot, chunk_pair, blocks, firsts, grads, actives, width, chunk):
    count = len(blocks)
    total = count * blocks[0].shape[0]
    hidden = grads[-1].shape[0]
    vmem = pl.BlockSpec(memory_space=pltpu.VMEM)
    smem = pl.BlockSpec(memory_space=pltpu.SMEM)
    return pl.pallas_call(
        functools.partial(cold_kernel, count, firsts, width),
        in_specs=[smem, smem] + [ANYWHERE] * (count + 2 * len(firsts)),
        out_specs=[vmem, vmem],
        out_shape=[jax.ShapeDtypeStruct((2, hidden, chunk), BF16)] * 2,
        scratch_shapes=[
            pltpu.VMEM((hidden, total), BF16),
            pltpu.VMEM((hidden, total), BF16),
            pltpu.VMEM((2, total, chunk), BF16),
            pltpu.VMEM((2, total, chunk), BF16),
            pltpu.SemaphoreType.DMA((2 * len(firsts),)),
            pltpu.SemaphoreType.DMA((2, 2, count)),
        ],
        compiler_params=call_params(),
        cost_estimate=small_cost(2),
        name="cold_weight_grads",
    )(hot, chunk_pair, *blocks, *grads, *actives)


def place_kernel(is_hot, flags_ref, *refs):
    values = refs[0] if is_hot else refs[:3]
    up_ref, down_ref, held, up, down, sems = refs[-6:]
    slot = flags_ref[0] if is_hot else 1 - flags_ref[0]
    if is_hot:
        fetch = pltpu.make_async_copy(values, held.at[0], sems.at[0])
        fetch.start()
        fetch.wait()
        up[...] = held[0, 0].T
        down[...] = held[0, 1]
    else:
        moved_ref, kept_ref, across_ref = values
        at_end = flags_ref[1] == 1

        @pl.when(at_end)
        def _():
            pltpu.make_async_copy(kept_ref, held.at[1], sems.at[1]).start()

        @pl.when(jnp.logical_not(at_end))
        def _():
            pltpu.make_async_copy(across_ref, held.at[1], sems.at[1]).start()

        fetch = pltpu.make_async_copy(moved_ref, held.at[0], sems.at[0])
        fetch.start()
        fetch.wait()
        pltpu.make_async_copy(across_ref, held.at[1], sems.at[1]).wait()
        total = (held[0].astype(F32) + held[1].astype(F32)).astype(BF16)
        up[...] = total[0].T
        down[...] = total[1]
    stores = [
        pltpu.make_async_copy(up, up_ref.at[slot], sems.at[2]),
        pltpu.make_async_copy(down, down_ref.at[slot], sems.at[3]),
    ]
    for store in stores:
        store.start()
    for store in stores:
        store.wait()


def place_call(flags, values, filled=()):
    hidden, chunk = values[0].shape[1:]
    is_hot = not filled
    shapes = [
        jax.ShapeDtypeStruct((2, chunk, hidden), BF16),
        jax.ShapeDtypeStruct((2, hidden, chunk), BF16),
    ]
    in_hbm = pl.BlockSpec(memory_space=pltpu.HBM)
    aliases = {} if is_hot else {1 + len(values): 0, 2 + len(values): 1}
    return pl.pallas_call(
        functools.partial(place_kernel, is_hot),
        in_specs=[pl.BlockSpec(memory_space=pltpu.SMEM)]
        + [in_hbm] * (len(values) + len(filled)),
        out_specs=[in_hbm] * 2,
        out_shape=shapes,
        input_output_aliases=aliases,
        scratch_shapes=[
            pltpu.VMEM((2, 2, hidden, chunk), BF16),
            pltpu.VMEM((chunk, hidden), BF16),
            pltpu.VMEM((hidden, chunk), BF16),
            pltpu.SemaphoreType.DMA((4,)),
        ],
        compiler_params=call_params(),
        cost_estimate=small_cost(),
        name="place_weight_grads",
    )(flags, *values, *filled)


class RowSums:
    def __init__(self, half, lefts, own, copied, outs, scratch, parts=None, pick=None, arrived=None):
        self.half, self.own, self.copied, self.outs = half, own, copied, outs
        self.parts, self.pick, self.arrived_ref = parts, pick, arrived
        self.is_output = parts is not None
        self.left, self.weights, self.out, *rest = scratch
        self.arrived = rest.pop(0) if arrived is not None else None
        left_sems, self.chunk_sems, self.out_sems = rest
        self.hidden, self.width = own.shape[1:] if self.is_output else own.shape[:0:-1]
        self.step = self.weights.shape[3] if self.is_output else self.weights.shape[2]
        self.chunks, self.slots = self.weights.shape[:2]
        self.tail = pl.ds(self.width, self.out.shape[1] - self.width)
        self.of_left = Fetches(left_sems)
        row, column = 0, 0
        for ref in lefts:
            count = ref.shape[1] // 2
            self.of_left.add(
                ref.at[:, pl.ds(half * count, count)],
                self.left.at[pl.ds(row, ref.shape[0]), pl.ds(column, count)],
            )
            row += ref.shape[0]
            if row == self.left.shape[0]:
                row, column = 0, column + count

    def columns(self, j):
        return pl.ds(pl.multiple_of(j * self.step, self.step), self.step)

    def chunk_copies(self, j):
        here = self.columns(j)
        found = []
        for slot in range(self.slots):
            source = self.copied.at[0] if slot == 0 else self.own.at[slot - 1]
            source = source.at[:, here] if self.is_output else source.at[here]
            found.append(
                pltpu.make_async_copy(
                    source, self.weights.at[j, slot], self.chunk_sems.at[j, slot]
                )
            )
        if self.arrived is not None:
            found.append(
                pltpu.make_async_copy(
                    self.arrived_ref.at[:, here],
                    self.arrived.at[:, here],
                    self.chunk_sems.at[j, self.slots],
                )
            )
        return found

    def tail_copies(self):
        if self.arrived is None or not self.is_output:
            return []
        return [
            pltpu.make_async_copy(
                self.arrived_ref.at[:, self.tail],
                self.arrived.at[:, self.tail],
                self.chunk_sems.at[self.chunks, 0],
            )
        ]

    def stores(self, here, number):
        rows = self.out.shape[0] // len(self.outs)
        return [
            pltpu.make_async_copy(
                self.out.at[pl.ds(i * rows, rows), here],
                ref.at[:, here],
                self.out_sems.at[number, i],
            )
            for i, ref in enumerate(self.outs)
        ]

    def store(self, here, number, values):
        if self.arrived is not None:
            values = values + self.arrived[:, here].astype(F32)
        self.out[:, here] = values.astype(BF16)
        for copy in self.stores(here, number):
            copy.start()

    def start(self):
        self.of_left.start()

        @pl.loop(0, self.chunks)
        def _(j):
            for copy in self.chunk_copies(j):
                copy.start()

        for copy in self.tail_copies():
            copy.start()

    def compute(self):
        self.of_left.wait(range(len(self.of_left.copies)))

        @pl.loop(0, self.chunks)
        def _(j):
            for copy in self.chunk_copies(j):
                copy.wait()
            if self.is_output:
                right = self.weights[j].reshape(self.slots * self.hidden, self.step)
                values = dot(self.left[...], right, (0, 0))
            else:
                right = jnp.concatenate(
                    [self.weights[j, slot] for slot in range(self.slots)], axis=1
                )
                values = dot(self.left[...], right, (0, 1))
            self.store(self.columns(j), j, values)

        if self.is_output:
            tables, stacked = [], []
            for ref in self.parts:
                count = ref.shape[1] // 2
                stacked.append(ref[:, self.half * count : (self.half + 1) * count])
                if sum(values.shape[0] for values in stacked) == self.pick.shape[0]:
                    tables.append(jnp.concatenate(stacked, axis=0))
                    stacked = []
            table = jnp.concatenate(tables, axis=1)
            for copy in self.tail_copies():
                copy.wait()
            self.store(self.tail, self.chunks, dot(table, self.pick[...], (0, 0)))

    def finish(self):
        @pl.loop(0, self.chunks)
        def _(j):
            for copy in self.stores(self.columns(j), j):
                copy.wait()

        if self.is_output:
            for copy in self.stores(self.tail, self.chunks):
                copy.wait()


def rows_kernel(half, pieces, with_arrived, *refs):
    def take(count):
        nonlocal refs
        found, refs = refs[:count], refs[count:]
        return found

    grads, actives, parts = take(pieces), take(pieces), take(pieces)
    up, copy_up, down, copy_down, pick = take(5)
    arrived = take(2) if with_arrived else (None, None)
    outs = 4 if with_arrived else 1
    gradient_outs, output_outs = take(outs), take(outs)
    scratch = 7 if with_arrived else 6
    gradient = RowSums(
        half, grads, up, copy_up, gradient_outs, take(scratch), arrived=arrived[0]
    )
    output = RowSums(
        half, actives, down, copy_down, output_outs, take(scratch), parts, pick, arrived[1]
    )
    for part in (gradient, output):
        part.start()
    for part in (gradient, output):
        part.compute()
    for part in (gradient, output):
        part.finish()


def rows_call(half, grads, actives, parts, weights, pick, arrived=()):
    own_up, own_down, copy_up, copy_down = weights
    slots = own_up.shape[0] + 1
    width, hidden = own_up.shape[1:]
    total = sum(a.shape[1] * a.shape[0] for a in grads) // (2 * slots * hidden)
    step = 512
    chunks = width // step
    outs = 4 if arrived else 1
    vmem = pl.BlockSpec(memory_space=pltpu.VMEM)
    operands = [*grads, *actives, *parts, own_up, copy_up, own_down, copy_down, pick, *arrived]
    in_specs = (
        [ANYWHERE] * (2 * len(grads))
        + [vmem] * len(parts)
        + [ANYWHERE] * 4
        + [vmem]
        + [ANYWHERE] * len(arrived)
    )
    out_shape, scratch = [], []
    for columns, tile in (
        (width, (step, hidden)),
        (width + pick.shape[1], (hidden, step)),
    ):
        out_shape += [jax.ShapeDtypeStruct((total // outs, columns), BF16)] * outs
        scratch += [
            pltpu.VMEM((slots * hidden, total), BF16),
            pltpu.VMEM((chunks, slots) + tile, BF16),
            pltpu.VMEM((total, columns), BF16),
        ]
        if arrived:
            scratch.append(pltpu.VMEM((total, columns), BF16))
        scratch += [
            pltpu.SemaphoreType.DMA((len(grads),)),
            pltpu.SemaphoreType.DMA((chunks + 1, slots + 1)),
            pltpu.SemaphoreType.DMA((chunks + 1, outs)),
        ]
    return pl.pallas_call(
        functools.partial(rows_kernel, half, len(grads), bool(arrived)),
        in_specs=in_specs,
        out_specs=[ANYWHERE] * len(out_shape),
        out_shape=out_shape,
        scratch_shapes=scratch,
        compiler_params=call_params(),
        cost_estimate=small_cost(),
        name="row_sums",
    )(*operands)


class CubeExchange:
    def __init__(self):
        self.first = [(i, i ^ (4 if i & 1 else 2)) for i in range(8)]
        self.second = [(i, i ^ (2 if i & 1 else 4)) for i in range(8)]
        self.mate = [(i, i ^ 1) for i in range(8)]

    def sources(self, me):
        first = jnp.where(me % 2 == 1, 4, 2)
        second = 6 - first
        zero = jnp.zeros_like(me)
        return me ^ jnp.stack(
            [zero, zero + 1, first, second, second + 1, first + 1, zero + 6, zero + 7]
        )

    def first_hop(self, block):
        return lax.ppermute(block, "expert", self.first)

    def far(self, first_block):
        return lax.ppermute(first_block, "expert", self.second)

    def to_mate(self, block):
        return lax.ppermute(block, "expert", self.mate)


class PlainExchange:
    def __init__(self, count):
        self.count = count

    def sources(self, me):
        return jnp.arange(self.count, dtype=jnp.int32)

    def gather(self, block):
        return lax.all_gather(block, "expert", tiled=True)

    def reduce(self, partial):
        return lax.psum_scatter(
            partial.astype(BF16), "expert", scatter_dimension=0, tiled=True
        ).astype(F32)


def local(
    tokens,
    cotangent,
    gate_weights,
    expert_ids,
    copy_pick,
    copy_expert,
    up_weight,
    down_weight,
    copy_up,
    copy_down,
):
    device_count = lax.axis_size("expert")
    me = lax.axis_index("expert")
    rows, width = tokens.shape
    chosen = expert_ids.shape[1]
    local_count = up_weight.shape[0]
    hidden = up_weight.shape[2]
    expert_count = local_count * device_count
    moved_most = 3 * (rows * chosen // expert_count) // 8
    moved_rows = padded(device_count * moved_most, 128)

    column_count = expert_count + device_count
    owner = expert_ids // local_count
    column = jnp.where(copy_pick == 1, expert_count + owner, expert_ids)
    hit = column[:, :, None] == jnp.arange(column_count, dtype=jnp.int32)
    gates = jnp.sum(jnp.where(hit, gate_weights[:, :, None], 0.0), axis=1)
    moved = jnp.sum(hit[:, :, expert_count:].astype(F32), axis=1)
    lower = (
        jnp.arange(rows, dtype=jnp.int32)[:, None] >= jnp.arange(rows, dtype=jnp.int32)[None, :]
    )
    rank = dot(lower.astype(BF16), moved.astype(BF16), (1, 0)) * moved
    gate_high, gate_low = split_two(gates)
    table_width = padded(2 * column_count + device_count, 128)
    table = jnp.concatenate(
        [
            gate_high,
            gate_low,
            rank.astype(BF16),
            jnp.zeros((rows, table_width - 2 * column_count - device_count), BF16),
        ],
        axis=1,
    )
    behind = (me + device_count - 1) % device_count
    columns = [local_count * me + i for i in range(local_count)] + [expert_count + behind]
    slots = len(columns)
    table_rows = jnp.arange(table_width, dtype=jnp.int32)
    wanted = jnp.stack(columns)
    high_pick = (table_rows[:, None] == wanted[None, :]).astype(BF16)
    low_pick = (table_rows[:, None] == wanted[None, :] + column_count).astype(BF16)
    wanted_rank = 2 * column_count + jnp.stack([behind, me])
    rank_pick = (table_rows[:, None] == wanted_rank[None, :]).astype(BF16)
    to_owner = [(i, (i - 1) % device_count) for i in range(device_count)]
    hot_slot = copy_expert[(me + 1) % device_count] % local_count
    own_width = local_count * hidden

    def finish(output_sum, gradient_sum, table_sum):
        grads = table_sum[:, :column_count] + table_sum[:, column_count : 2 * column_count]
        gate_grad = jnp.sum(jnp.where(hit, grads[:, None, :], 0.0), axis=2)
        return output_sum.astype(BF16), gradient_sum.astype(BF16), gate_grad

    replicas = lax.axis_size("dp")
    if device_count == 8 and local_count == 2 and replicas == 4:
        exchange = CubeExchange()
        replica = lax.axis_index("dp")
        hot = hot_slot.reshape(1).astype(jnp.int32)
        cold_column = local_count * me + 1 - hot_slot
        weights = (up_weight, down_weight, copy_up, copy_down)
        base = jnp.repeat((exchange.sources(me) * moved_most).astype(F32), rows)[None, :]
        slot_columns = jnp.stack([wanted[slots - 1], wanted[0], wanted[1]])
        pick_columns = jnp.stack(
            [wanted[slots - 1], wanted[0], wanted[1], wanted_rank[0], wanted_rank[1], cold_column]
            + [jnp.int32(-1)] * 10
        )
        is_gate = jnp.array([1, 1, 1, 0, 0, 1] + [0] * 10, jnp.int32)
        pick = (
            (table_rows[None, :] == pick_columns[:, None])
            | (
                (table_rows[None, :] == pick_columns[:, None] + column_count)
                & (is_gate[:, None] == 1)
            )
        ).astype(BF16)
        part_columns = jnp.stack(
            [slot_columns, slot_columns + column_count] + [jnp.full((slots,), -1, jnp.int32)] * 14,
            axis=1,
        ).reshape(-1)
        part_pick = (table_rows[None, :] == part_columns[:, None]).astype(BF16)

        own = jnp.concatenate([tokens, cotangent, table], axis=1)
        own_mate = exchange.to_mate(own)
        a, b = exchange.first_hop(own), exchange.far(own)
        replica_pairs = [(0, 1), (1, 0), (2, 3), (3, 2)]
        other = lax.ppermute(own, "dp", replica_pairs)
        blocks_1 = [own, own_mate]
        ends = (2 * rows, 6 * rows)
        grad_1, active_1, part_1, place_1, packed = hidden_call(
            hot, blocks_1, weights, pick, base[:, : ends[0]], (COPY, 0, 1), moved_rows
        )
        a, b, grad_1 = lax.optimization_barrier((a, b, grad_1))
        d = exchange.far(a)
        a_mate = exchange.to_mate(a)
        other, a_mate = lax.optimization_barrier((other, a_mate))
        blocks_2 = [a, b, a_mate, exchange.to_mate(b)]
        grad_2, active_2, part_2, place_2, packed = hidden_call(
            hot, blocks_2, weights, pick, base[:, ends[0] : ends[1]], (COPY, 0, 1), moved_rows,
            packed,
        )
        grad_2, d = lax.optimization_barrier((grad_2, d))
        blocks_3 = [d, exchange.to_mate(d)]
        blocks = blocks_1 + blocks_2 + blocks_3

        other_a = exchange.first_hop(other)

        late_base = base[:, ends[1] :]
        grad_copy, active_copy, part_copy, place_3, packed = hidden_call(
            hot, blocks_3, weights, pick, late_base, (COPY,), moved_rows, packed
        )
        packed = lax.ppermute(packed, "expert", to_owner)
        grad_3, active_3, part_3 = hidden_call(hot, blocks_3, weights, pick, late_base, (0, 1))
        packed, grad_3, other, other_a = lax.optimization_barrier(
            (packed, grad_3, other, other_a)
        )
        other_b = exchange.far(other)
        other_d = exchange.far(other_a)
        hot_grads = hot_call(
            hot, blocks, (1, 1, 0), (grad_1, grad_2, grad_3), (active_1, active_2, active_3),
            (place_1, place_2, place_3), packed, width, replicas,
        )
        hot_sum = lax.psum_scatter(hot_grads, "dp", scatter_dimension=0, tiled=True)[0]

        grad_3, active_3, _ = lax.optimization_barrier((grad_3, active_3, hot_grads))
        sides = (
            (grad_1, grad_2, grad_copy, grad_3),
            (active_1, active_2, active_copy, active_3),
            (part_1, part_2, part_copy, part_3),
            weights, part_pick,
        )
        mates_rows = rows_call(1, *sides)
        *mates_rows, other_b = lax.optimization_barrier((*mates_rows, other_b))
        arrived = [exchange.to_mate(block) for block in mates_rows]
        own_rows = rows_call(0, *sides, tuple(arrived))
        gradient_rows, output_rows = own_rows[:4], own_rows[4:]
        other_d, _ = lax.optimization_barrier((other_d, own_rows[0]))
        pair_blocks = [other, other_a, other_b, other_d]
        pair_blocks = pair_blocks + [exchange.to_mate(block) for block in pair_blocks]
        from_diagonal = [exchange.far(rows_of[3]) for rows_of in (gradient_rows, output_rows)]
        grad_pair, active_pair = hidden_call(hot, pair_blocks, weights, pick, base, (COLD,))
        grad_pair, *from_diagonal = lax.optimization_barrier((grad_pair, *from_diagonal))
        chunk_pairs = jnp.array([[1, 0], [3, 2], [0, 1], [2, 3]], jnp.int32)
        given, second = cold_call(
            hot, chunk_pairs[replica], blocks + pair_blocks, (1, 1, 0, None),
            (grad_1, grad_2, grad_3, grad_pair), (active_1, active_2, active_3, active_pair),
            width, width // replicas,
        )
        at_end = (replica == 0) | (replica == replicas - 1)
        flags = jnp.stack([hot_slot, at_end.astype(jnp.int32)]).astype(jnp.int32)
        filled = place_call(flags, [hot_sum])
        *from_diagonal, first_filled = lax.optimization_barrier((*from_diagonal, filled[0]))
        filled = (first_filled, filled[1])
        relayed = [
            (rows_of[1].astype(F32) + arrived.astype(F32)).astype(BF16)
            for rows_of, arrived in zip((gradient_rows, output_rows), from_diagonal)
        ]
        moved = lax.ppermute(given, "dp", [(0, 1), (1, 3), (2, 0), (3, 2)])
        hops = [exchange.far(rows_of[2]) for rows_of in (gradient_rows, output_rows)]
        gradient_hop, output_hop = (exchange.first_hop(block) for block in relayed)
        moved, to_middle, gradient_hop, *hops = lax.optimization_barrier(
            (moved, second, gradient_hop, *hops)
        )
        gradient_sum, output_sum = (
            rows_of[0].astype(F32) + first.astype(F32) + other_hop.astype(F32)
            for rows_of, first, other_hop in zip(
                (gradient_rows, output_rows), (gradient_hop, output_hop), hops
            )
        )
        across = lax.ppermute(to_middle, "dp", [(1, 2), (2, 1)])
        up_grad, down_grad = place_call(flags, [moved, second, across], filled)
        return (*finish(output_sum[:, :width], gradient_sum, output_sum[:, width:]), up_grad, down_grad)

    exchange = PlainExchange(device_count)
    up_all = jnp.concatenate([up_weight[i] for i in range(local_count)] + [copy_up[0]], axis=1)
    down_all = jnp.concatenate(
        [down_weight[i] for i in range(local_count)] + [copy_down[0]], axis=0
    )

    def some_rows(own_block):
        gathered = exchange.gather(own_block)
        all_tokens = gathered[:, :width]
        all_cotangent = gathered[:, width : 2 * width]
        all_table = gathered[:, 2 * width :]
        slot_gates = dot(all_table, high_pick + low_pick, (1, 0))
        ranks = dot(all_table, rank_pick, (1, 0)).astype(jnp.int32)
        base = jnp.repeat(exchange.sources(me) * moved_most, own_block.shape[0])
        place = jnp.where(ranks > 0, base[:, None] + ranks - 1, -1)
        moved_index = jnp.arange(moved_rows, dtype=jnp.int32)[None, :]
        served_place = (place[:, :1] == moved_index).astype(BF16)
        owned_place = (place[:, 1:] == moved_index).astype(BF16)
        linear = dot(all_tokens, up_all, (1, 0))
        raw_grad = dot(all_cotangent, down_all, (1, 1))
        spread = jnp.repeat(slot_gates, hidden, axis=1)
        sigma = jax.nn.sigmoid(linear)
        active = (linear * sigma).astype(BF16).astype(F32)
        gate_part = jnp.sum((active * raw_grad).reshape(-1, slots, hidden), axis=2)
        weighted = (spread * active).astype(BF16)
        slope = sigma * (1.0 + linear * (1.0 - sigma))
        linear_grad = (spread * raw_grad * slope).astype(BF16)
        both = jnp.concatenate([linear_grad[:, own_width:], weighted[:, own_width:]], axis=1)
        packed = dot(served_place, both, (0, 0)).astype(BF16)
        packed = lax.ppermute(packed, "expert", to_owner)
        unpacked = dot(owned_place, packed, (1, 0)).astype(BF16)
        up_parts = []
        down_parts = []
        for i in range(local_count):
            here = (hot_slot == i).astype(BF16)
            part = slice(i * hidden, (i + 1) * hidden)
            total_grad = linear_grad[:, part] + unpacked[:, :hidden] * here
            total_active = weighted[:, part] + unpacked[:, hidden:] * here
            up_parts.append(dot(all_tokens, total_grad, (0, 0)))
            down_parts.append(dot(total_active, all_cotangent, (0, 0)))
        mixed = dot(weighted, down_all, (1, 0)).astype(BF16)
        back = dot(linear_grad, up_all, (1, 1)).astype(BF16)
        part_high, part_low = split_two(gate_part)
        grad_table = dot(part_high, high_pick, (1, 1)) + dot(part_low, low_pick, (1, 1))
        summed = exchange.reduce(
            jnp.concatenate([mixed, back, grad_table.astype(BF16)], axis=1)
        )
        return summed, jnp.stack(up_parts), jnp.stack(down_parts)

    own = jnp.concatenate([tokens, cotangent, table], axis=1)
    pieces = max(1, device_count // 8)
    if pieces == 1:
        summed, up_sum, down_sum = some_rows(own)
    else:

        def step(totals, piece):
            summed, up_part, down_part = some_rows(piece)
            return (totals[0] + up_part, totals[1] + down_part), summed

        zeros = (jnp.zeros(up_weight.shape, F32), jnp.zeros(down_weight.shape, F32))
        (up_sum, down_sum), summed = lax.scan(
            step, zeros, own.reshape(pieces, rows // pieces, own.shape[1])
        )
        summed = summed.reshape(rows, own.shape[1])
    up_grad = lax.psum_scatter(up_sum.astype(BF16), "dp", scatter_dimension=1, tiled=True)
    down_grad = lax.psum_scatter(down_sum.astype(BF16), "dp", scatter_dimension=2, tiled=True)
    parts = (summed[:, :width], summed[:, width : 2 * width], summed[:, 2 * width :])
    return (*finish(*parts), up_grad, down_grad)


def solution(mesh):
    placed = (
        P(("expert", "dp"), None),
        P(("expert", "dp"), None),
        P(("expert", "dp"), None),
        P(("expert", "dp"), None),
        P(("expert", "dp"), None),
        P(),
        P("expert", None, None),
        P("expert", None, None),
        P("expert", None, None),
        P("expert", None, None),
    )
    return jax.shard_map(
        local,
        mesh=mesh,
        in_specs=placed,
        out_specs=(
            P(("expert", "dp"), None),
            P(("expert", "dp"), None),
            P(("expert", "dp"), None),
            P("expert", "dp", None),
            P("expert", None, "dp"),
        ),
        check_vma=False,
    )
```

```python
import functools

import jax
import jax.numpy as jnp
from jax import lax
from jax.experimental import pallas as pl
from jax.experimental.pallas import tpu as pltpu
from jax.sharding import PartitionSpec as P

BF16 = jnp.bfloat16
F32 = jnp.float32


def padded(count, multiple):
    return -(-count // multiple) * multiple


def dot(a, b, contract):
    return lax.dot_general(a, b, ((contract[:1], contract[1:]), ((), ())), preferred_element_type=F32)


def split_two(values):
    high = values.astype(BF16)
    return high, (values - high.astype(F32)).astype(BF16)


VMEM_LIMIT = 64 * 1024 * 1024
ANYWHERE = pl.BlockSpec(memory_space=pl.ANY)


def call_params():
    return pltpu.CompilerParams(vmem_limit_bytes=VMEM_LIMIT)


def small_cost(microseconds=0):
    return pl.CostEstimate(
        flops=1 + int(microseconds * 1e9),
        bytes_accessed=1 + int(microseconds * 3e6),
        transcendentals=0,
    )


class Fetches:
    def __init__(self, sems):
        self.sems = sems
        self.copies = []

    def add(self, source, target):
        self.copies.append(
            pltpu.make_async_copy(source, target, self.sems.at[len(self.copies)])
        )
        return len(self.copies) - 1

    def start(self):
        for copy in self.copies:
            copy.start()

    def wait(self, numbers):
        for number in numbers:
            self.copies[number].wait()


COPY, COLD = "copy", "cold"
SERVED_RANK, OWNED_RANK, COLD_GATE = 3, 4, 5


def hidden_kernel(blocks, slots, packing, width, *refs):
    hot_ref, refs = refs[0], refs[1:]
    row_refs, refs = refs[:blocks], refs[blocks:]
    up_ref, down_ref, copy_up_ref, copy_down_ref, pick_ref, base_ref, *refs = refs
    before_ref = refs.pop(0) if packing == 2 else None
    grad_ref, active_ref, *refs = refs
    part_ref = refs.pop(0) if COLD not in slots else None
    place_ref, packed_ref = (refs.pop(0), refs.pop(0)) if packing else (None, None)
    together, ups, downs, slot_sems, block_sems = refs
    gates = {}
    rows = row_refs[0].shape[0]
    hidden = down_ref.shape[1]
    group = 2 * rows

    def slot_copies(number, slot):
        index = 0 if slot == COPY else (1 - hot_ref[0] if slot == COLD else slot)
        up, down = (copy_up_ref, copy_down_ref) if slot == COPY else (up_ref, down_ref)
        return [
            pltpu.make_async_copy(up.at[index], ups.at[number], slot_sems.at[number, 0]),
            pltpu.make_async_copy(down.at[index], downs.at[number], slot_sems.at[number, 1]),
        ]

    block_copies = [
        pltpu.make_async_copy(ref, together.at[pl.ds(i * rows, rows)], block_sems.at[i])
        for i, ref in enumerate(row_refs)
    ]
    for copy in slot_copies(0, slots[0]) + block_copies:
        copy.start()
    for number in range(1, len(slots)):
        for copy in slot_copies(number, slots[number]):
            copy.start()
    first_gate = 0 if slots[0] == COPY else (COLD_GATE if slots[0] == COLD else 1)

    for number, slot in enumerate(slots):
        for copy in slot_copies(number, slot):
            copy.wait()
        to = pl.ds(number * hidden, hidden)

        for g in range(blocks // 2):
            here = slice(g * group, (g + 1) * group)
            if number == 0:
                for copy in block_copies[2 * g : 2 * g + 2]:
                    copy.wait()
                found = dot(pick_ref[...], together[here, 2 * width :], (1, 1))
                gates[g] = found
                if packing:
                    ranks = found[SERVED_RANK : OWNED_RANK + 1]
                    place = jnp.where(ranks > 0.5, base_ref[:, here] + ranks - 1.0, -1.0)
                    place_ref[:, here] = jnp.concatenate(
                        [place, jnp.zeros((6, group), F32)], axis=0
                    )
            gate = gates[g][first_gate + number : first_gate + number + 1]
            linear = dot(ups[number], together[here, :width], (0, 1))
            raw_grad = dot(downs[number], together[here, width : 2 * width], (1, 1))
            sigma = 0.5 * jnp.tanh(0.5 * linear) + 0.5
            active = (linear * sigma).astype(BF16).astype(F32)
            if part_ref is not None:
                part = jnp.sum(active * raw_grad, axis=0, keepdims=True)
                part_high, part_low = split_two(part)
                part_ref[pl.ds(16 * number, 16), here] = jnp.concatenate(
                    [part_high, part_low, jnp.zeros((14, group), BF16)], axis=0
                )
            active_ref[to, here] = (gate * active).astype(BF16)
            slope = sigma * (1.0 + linear * (1.0 - sigma))
            grad_ref[to, here] = (gate * raw_grad * slope).astype(BF16)

    if packing:
        moved_rows = packed_ref.shape[1]
        index = lax.broadcasted_iota(jnp.int32, (moved_rows, blocks * rows), 0)
        chosen = (index == place_ref[0:1, :].astype(jnp.int32)).astype(F32).astype(BF16)
        for half, ref in enumerate((grad_ref, active_ref)):
            to = slice(half * hidden, (half + 1) * hidden)
            found = dot(ref[:hidden, :], chosen, (1, 1))
            if before_ref is not None:
                found = found + before_ref[to, :].astype(F32)
            packed_ref[to, :] = found.astype(BF16)


def hidden_call(hot, blocks, weights, pick, base, slots, moved_rows=0, before=None):
    count = len(blocks)
    rows, columns = blocks[0].shape
    width, hidden = weights[0].shape[1:]
    total = count * rows
    packing = 0 if moved_rows == 0 else (1 if before is None else 2)
    vmem = pl.BlockSpec(memory_space=pltpu.VMEM)
    operands = [hot, *blocks, *weights, pick, base]
    in_specs = [pl.BlockSpec(memory_space=pltpu.SMEM)] + [ANYWHERE] * (count + 4) + [vmem] * 2
    if packing == 2:
        operands.append(before)
        in_specs.append(vmem)
    out_shape = [jax.ShapeDtypeStruct((len(slots) * hidden, total), BF16)] * 2
    if COLD not in slots:
        out_shape.append(jax.ShapeDtypeStruct((len(slots) * 16, total), BF16))
    if packing:
        out_shape.append(jax.ShapeDtypeStruct((8, total), F32))
        out_shape.append(jax.ShapeDtypeStruct((2 * hidden, moved_rows), BF16))
    return pl.pallas_call(
        functools.partial(hidden_kernel, count, slots, packing, width),
        in_specs=in_specs,
        out_specs=[vmem] * len(out_shape),
        out_shape=out_shape,
        scratch_shapes=[
            pltpu.VMEM((total, columns), BF16),
            pltpu.VMEM((len(slots), width, hidden), BF16),
            pltpu.VMEM((len(slots), hidden, width), BF16),
            pltpu.SemaphoreType.DMA((len(slots), 2)),
            pltpu.SemaphoreType.DMA((count,)),
        ],
        compiler_params=call_params(),
        cost_estimate=small_cost(2 if COLD in slots else 0),
        name="hidden_units",
    )(*operands)


def fetch_pieces(fetches, pieces, expert, target):
    hidden = target.shape[0]
    found, column = [], 0
    for piece, first in pieces:
        count = piece.shape[1]
        source = piece
        if first is not None:
            start = pl.multiple_of((first + expert) * hidden, hidden)
            source = piece.at[pl.ds(start, hidden)]
        found.append(fetches.add(source, target.at[:, pl.ds(column, count)]))
        column += count
    return found


def chunk_copies_of(row_refs, tokens, cotan, width, sems):
    rows, chunk = row_refs[0].shape[0], tokens.shape[2]

    def copies(place, number, half):
        columns = pl.ds(pl.multiple_of(half * width + number * chunk, chunk), chunk)
        target = (tokens, cotan)[half]
        return [
            pltpu.make_async_copy(
                ref.at[:, columns],
                target.at[place, pl.ds(i * rows, rows)],
                sems.at[place, half, i],
            )
            for i, ref in enumerate(row_refs)
        ]

    return copies


def hot_kernel(blocks, firsts, width, *refs):
    hot_ref, refs = refs[0], refs[1:]
    row_refs, refs = refs[:blocks], refs[blocks:]
    pieces = len(firsts)
    grad_refs, active_refs, place_refs, refs = (
        refs[:pieces], refs[pieces : 2 * pieces], refs[2 * pieces : 3 * pieces], refs[3 * pieces :]
    )
    packed_ref, out_ref, grads, actives, tokens, cotan, out, sems, chunk_sems, out_sems = refs
    chunks, total, chunk = tokens.shape
    hidden = grads.shape[0]
    fetches = Fetches(sems)
    of_rows = []
    for sources, target in ((grad_refs, grads), (active_refs, actives)):
        of_rows.append(fetch_pieces(fetches, list(zip(sources, firsts)), hot_ref[0], target))
    chunk_copies = chunk_copies_of(row_refs, tokens, cotan, width, chunk_sems)
    fetches.start()

    @pl.loop(0, chunks)
    def _(j):
        for copy in chunk_copies(j, j, 0) + chunk_copies(j, j, 1):
            copy.start()

    def store_of(j):
        return pltpu.make_async_copy(out.at[j], out_ref.at[j], out_sems.at[j])

    place = jnp.concatenate([ref[1:2, :] for ref in place_refs], axis=1)
    index = lax.broadcasted_iota(jnp.int32, (packed_ref.shape[1], total), 0)
    chosen = (index == place.astype(jnp.int32)).astype(F32).astype(BF16)
    for half, target in enumerate((grads, actives)):
        fetches.wait(of_rows[half])
        spread = dot(packed_ref[half * hidden : (half + 1) * hidden, :], chosen, (1, 0))
        target[...] = (target[...].astype(F32) + spread).astype(BF16)

    @pl.loop(0, chunks)
    def _(j):
        for half, (left, right) in enumerate(((grads, tokens), (actives, cotan))):
            for copy in chunk_copies(j, j, half):
                copy.wait()
            out[j, half] = dot(left[...], right[j], (1, 0)).astype(BF16)
        store_of(j).start()

    @pl.loop(0, chunks)
    def _(j):
        store_of(j).wait()


def hot_call(hot, blocks, firsts, grads, actives, places, packed, width, chunks):
    count = len(blocks)
    total = count * blocks[0].shape[0]
    chunk = width // chunks
    hidden = packed.shape[0] // 2
    vmem = pl.BlockSpec(memory_space=pltpu.VMEM)
    return pl.pallas_call(
        functools.partial(hot_kernel, count, firsts, width),
        in_specs=[pl.BlockSpec(memory_space=pltpu.SMEM)]
        + [ANYWHERE] * (count + 2 * len(firsts))
        + [vmem] * (len(firsts) + 1),
        out_specs=ANYWHERE,
        out_shape=jax.ShapeDtypeStruct((chunks, 2, hidden, chunk), BF16),
        scratch_shapes=[
            pltpu.VMEM((hidden, total), BF16),
            pltpu.VMEM((hidden, total), BF16),
            pltpu.VMEM((chunks, total, chunk), BF16),
            pltpu.VMEM((chunks, total, chunk), BF16),
            pltpu.VMEM((chunks, 2, hidden, chunk), BF16),
            pltpu.SemaphoreType.DMA((2 * len(firsts),)),
            pltpu.SemaphoreType.DMA((chunks, 2, count)),
            pltpu.SemaphoreType.DMA((chunks,)),
        ],
        compiler_params=call_params(),
        cost_estimate=small_cost(),
        name="hot_weight_grads",
    )(hot, *blocks, *grads, *actives, *places, packed)


def cold_kernel(blocks, firsts, width, *refs):
    hot_ref, chunk_ref, refs = refs[0], refs[1], refs[2:]
    row_refs, refs = refs[:blocks], refs[blocks:]
    pieces = len(firsts)
    grad_refs, active_refs, refs = refs[:pieces], refs[pieces : 2 * pieces], refs[2 * pieces :]
    near_ref, far_ref, grads, actives, tokens, cotan, sems, chunk_sems = refs
    fetches = Fetches(sems)
    of_rows = []
    for sources, target in ((grad_refs, grads), (active_refs, actives)):
        of_rows.append(fetch_pieces(fetches, list(zip(sources, firsts)), 1 - hot_ref[0], target))
    chunk_copies = chunk_copies_of(row_refs, tokens, cotan, width, chunk_sems)
    fetches.start()

    @pl.loop(0, 2)
    def _(j):
        for copy in chunk_copies(j, chunk_ref[j], 0) + chunk_copies(j, chunk_ref[j], 1):
            copy.start()

    for j, out_ref in enumerate((near_ref, far_ref)):
        for half, (left, right) in enumerate(((grads, tokens), (actives, cotan))):
            if j == 0:
                fetches.wait(of_rows[half])
            for copy in chunk_copies(j, chunk_ref[j], half):
                copy.wait()
            out_ref[half] = dot(left[...], right[j], (1, 0)).astype(BF16)


def cold_call(hot, chunk_pair, blocks, firsts, grads, actives, width, chunk):
    count = len(blocks)
    total = count * blocks[0].shape[0]
    hidden = grads[-1].shape[0]
    vmem = pl.BlockSpec(memory_space=pltpu.VMEM)
    smem = pl.BlockSpec(memory_space=pltpu.SMEM)
    return pl.pallas_call(
        functools.partial(cold_kernel, count, firsts, width),
        in_specs=[smem, smem] + [ANYWHERE] * (count + 2 * len(firsts)),
        out_specs=[vmem, vmem],
        out_shape=[jax.ShapeDtypeStruct((2, hidden, chunk), BF16)] * 2,
        scratch_shapes=[
            pltpu.VMEM((hidden, total), BF16),
            pltpu.VMEM((hidden, total), BF16),
            pltpu.VMEM((2, total, chunk), BF16),
            pltpu.VMEM((2, total, chunk), BF16),
            pltpu.SemaphoreType.DMA((2 * len(firsts),)),
            pltpu.SemaphoreType.DMA((2, 2, count)),
        ],
        compiler_params=call_params(),
        cost_estimate=small_cost(2),
        name="cold_weight_grads",
    )(hot, chunk_pair, *blocks, *grads, *actives)


def place_kernel(is_hot, flags_ref, *refs):
    values = refs[0] if is_hot else refs[:3]
    up_ref, down_ref, held, up, down, sems = refs[-6:]
    slot = flags_ref[0] if is_hot else 1 - flags_ref[0]
    if is_hot:
        fetch = pltpu.make_async_copy(values, held.at[0], sems.at[0])
        fetch.start()
        fetch.wait()
        up[...] = held[0, 0].T
        down[...] = held[0, 1]
    else:
        moved_ref, kept_ref, across_ref = values
        at_end = flags_ref[1] == 1
        for half in range(2):

            @pl.when(at_end)
            def _(half=half):
                pltpu.make_async_copy(
                    kept_ref.at[half], held.at[1, half], sems.at[4 + half]
                ).start()

            @pl.when(jnp.logical_not(at_end))
            def _(half=half):
                pltpu.make_async_copy(
                    across_ref.at[half], held.at[1, half], sems.at[4 + half]
                ).start()

            pltpu.make_async_copy(moved_ref.at[half], held.at[0, half], sems.at[half]).start()
        for half, (target, out) in enumerate(((up, up_ref), (down, down_ref))):
            pltpu.make_async_copy(moved_ref.at[half], held.at[0, half], sems.at[half]).wait()
            pltpu.make_async_copy(across_ref.at[half], held.at[1, half], sems.at[4 + half]).wait()
            total = (held[0, half].astype(F32) + held[1, half].astype(F32)).astype(BF16)
            target[...] = total.T if half == 0 else total
            pltpu.make_async_copy(target, out.at[slot], sems.at[2 + half]).start()
        for half, (target, out) in enumerate(((up, up_ref), (down, down_ref))):
            pltpu.make_async_copy(target, out.at[slot], sems.at[2 + half]).wait()
        return
    stores = [
        pltpu.make_async_copy(up, up_ref.at[slot], sems.at[2]),
        pltpu.make_async_copy(down, down_ref.at[slot], sems.at[3]),
    ]
    for store in stores:
        store.start()
    for store in stores:
        store.wait()


def place_call(flags, values, filled=()):
    hidden, chunk = values[0].shape[1:]
    is_hot = not filled
    shapes = [
        jax.ShapeDtypeStruct((2, chunk, hidden), BF16),
        jax.ShapeDtypeStruct((2, hidden, chunk), BF16),
    ]
    aliases = {} if is_hot else {1 + len(values): 0, 2 + len(values): 1}
    return pl.pallas_call(
        functools.partial(place_kernel, is_hot),
        in_specs=[pl.BlockSpec(memory_space=pltpu.SMEM)]
        + [ANYWHERE] * (len(values) + len(filled)),
        out_specs=[ANYWHERE] * 2,
        out_shape=shapes,
        input_output_aliases=aliases,
        scratch_shapes=[
            pltpu.VMEM((2, 2, hidden, chunk), BF16),
            pltpu.VMEM((chunk, hidden), BF16),
            pltpu.VMEM((hidden, chunk), BF16),
            pltpu.SemaphoreType.DMA((6,)),
        ],
        compiler_params=pltpu.CompilerParams(vmem_limit_bytes=16 * 1024 * 1024),
        cost_estimate=small_cost(),
        name="place_weight_grads",
    )(flags, *values, *filled)


class RowSums:
    def __init__(self, half, lefts, own, copied, outs, scratch, parts=None, pick=None, arrived=None):
        self.half, self.own, self.copied, self.outs = half, own, copied, outs
        self.parts, self.pick, self.arrived_ref = parts, pick, arrived
        self.is_output = parts is not None
        self.left, self.weights, self.out, *rest = scratch
        self.arrived = rest.pop(0) if arrived is not None else None
        left_sems, self.chunk_sems, self.out_sems = rest
        self.hidden, self.width = own.shape[1:] if self.is_output else own.shape[:0:-1]
        self.step = self.weights.shape[3] if self.is_output else self.weights.shape[2]
        self.chunks, self.slots = self.weights.shape[:2]
        self.tail = pl.ds(self.width, self.out.shape[1] - self.width)
        self.of_left = Fetches(left_sems)
        row, column = 0, 0
        for ref in lefts:
            count = ref.shape[1] // 2
            self.of_left.add(
                ref.at[:, pl.ds(half * count, count)],
                self.left.at[pl.ds(row, ref.shape[0]), pl.ds(column, count)],
            )
            row += ref.shape[0]
            if row == self.left.shape[0]:
                row, column = 0, column + count

    def columns(self, j):
        return pl.ds(pl.multiple_of(j * self.step, self.step), self.step)

    def chunk_copies(self, j):
        here = self.columns(j)
        found = []
        for slot in range(self.slots):
            source = self.copied.at[0] if slot == 0 else self.own.at[slot - 1]
            source = source.at[:, here] if self.is_output else source.at[here]
            found.append(
                pltpu.make_async_copy(
                    source, self.weights.at[j, slot], self.chunk_sems.at[j, slot]
                )
            )
        if self.arrived is not None:
            found.append(
                pltpu.make_async_copy(
                    self.arrived_ref.at[:, here],
                    self.arrived.at[:, here],
                    self.chunk_sems.at[j, self.slots],
                )
            )
        return found

    def tail_copies(self):
        if self.arrived is None or not self.is_output:
            return []
        return [
            pltpu.make_async_copy(
                self.arrived_ref.at[:, self.tail],
                self.arrived.at[:, self.tail],
                self.chunk_sems.at[self.chunks, 0],
            )
        ]

    def stores(self, here, number):
        rows = self.out.shape[0] // len(self.outs)
        return [
            pltpu.make_async_copy(
                self.out.at[pl.ds(i * rows, rows), here],
                ref.at[:, here],
                self.out_sems.at[number, i],
            )
            for i, ref in enumerate(self.outs)
        ]

    def store(self, here, number, values):
        if self.arrived is not None:
            values = values + self.arrived[:, here].astype(F32)
        self.out[:, here] = values.astype(BF16)
        for copy in self.stores(here, number):
            copy.start()

    def start(self):
        self.of_left.start()

        @pl.loop(0, self.chunks)
        def _(j):
            for copy in self.chunk_copies(j):
                copy.start()

        for copy in self.tail_copies():
            copy.start()

    def compute(self):
        self.of_left.wait(range(len(self.of_left.copies)))

        @pl.loop(0, self.chunks)
        def _(j):
            for copy in self.chunk_copies(j):
                copy.wait()
            if self.is_output:
                right = self.weights[j].reshape(self.slots * self.hidden, self.step)
                values = dot(self.left[...], right, (0, 0))
            else:
                right = jnp.concatenate(
                    [self.weights[j, slot] for slot in range(self.slots)], axis=1
                )
                values = dot(self.left[...], right, (0, 1))
            self.store(self.columns(j), j, values)

        if self.is_output:
            tables, stacked = [], []
            for ref in self.parts:
                count = ref.shape[1] // 2
                stacked.append(ref[:, self.half * count : (self.half + 1) * count])
                if sum(values.shape[0] for values in stacked) == self.pick.shape[0]:
                    tables.append(jnp.concatenate(stacked, axis=0))
                    stacked = []
            table = jnp.concatenate(tables, axis=1)
            for copy in self.tail_copies():
                copy.wait()
            self.store(self.tail, self.chunks, dot(table, self.pick[...], (0, 0)))

    def finish(self):
        @pl.loop(0, self.chunks)
        def _(j):
            for copy in self.stores(self.columns(j), j):
                copy.wait()

        if self.is_output:
            for copy in self.stores(self.tail, self.chunks):
                copy.wait()


def rows_kernel(half, pieces, with_arrived, *refs):
    def take(count):
        nonlocal refs
        found, refs = refs[:count], refs[count:]
        return found

    grads, actives, parts = take(pieces), take(pieces), take(pieces)
    up, copy_up, down, copy_down, pick = take(5)
    arrived = take(2) if with_arrived else (None, None)
    outs = 4 if with_arrived else 1
    gradient_outs, output_outs = take(outs), take(outs)
    scratch = 7 if with_arrived else 6
    gradient = RowSums(
        half, grads, up, copy_up, gradient_outs, take(scratch), arrived=arrived[0]
    )
    output = RowSums(
        half, actives, down, copy_down, output_outs, take(scratch), parts, pick, arrived[1]
    )
    for part in (gradient, output):
        part.start()
    for part in (gradient, output):
        part.compute()
    for part in (gradient, output):
        part.finish()


def rows_call(half, grads, actives, parts, weights, pick, arrived=()):
    own_up, own_down, copy_up, copy_down = weights
    slots = own_up.shape[0] + 1
    width, hidden = own_up.shape[1:]
    total = sum(a.shape[1] * a.shape[0] for a in grads) // (2 * slots * hidden)
    step = 512
    chunks = width // step
    outs = 4 if arrived else 1
    vmem = pl.BlockSpec(memory_space=pltpu.VMEM)
    operands = [*grads, *actives, *parts, own_up, copy_up, own_down, copy_down, pick, *arrived]
    in_specs = (
        [ANYWHERE] * (2 * len(grads))
        + [vmem] * len(parts)
        + [ANYWHERE] * 4
        + [vmem]
        + [ANYWHERE] * len(arrived)
    )
    out_shape, scratch = [], []
    for columns, tile in (
        (width, (step, hidden)),
        (width + pick.shape[1], (hidden, step)),
    ):
        out_shape += [jax.ShapeDtypeStruct((total // outs, columns), BF16)] * outs
        scratch += [
            pltpu.VMEM((slots * hidden, total), BF16),
            pltpu.VMEM((chunks, slots) + tile, BF16),
            pltpu.VMEM((total, columns), BF16),
        ]
        if arrived:
            scratch.append(pltpu.VMEM((total, columns), BF16))
        scratch += [
            pltpu.SemaphoreType.DMA((len(grads),)),
            pltpu.SemaphoreType.DMA((chunks + 1, slots + 1)),
            pltpu.SemaphoreType.DMA((chunks + 1, outs)),
        ]
    return pl.pallas_call(
        functools.partial(rows_kernel, half, len(grads), bool(arrived)),
        in_specs=in_specs,
        out_specs=[ANYWHERE] * len(out_shape),
        out_shape=out_shape,
        scratch_shapes=scratch,
        compiler_params=call_params(),
        cost_estimate=small_cost(),
        name="row_sums",
    )(*operands)


class CubeExchange:
    def __init__(self):
        self.first = [(i, i ^ (4 if i & 1 else 2)) for i in range(8)]
        self.second = [(i, i ^ (2 if i & 1 else 4)) for i in range(8)]
        self.mate = [(i, i ^ 1) for i in range(8)]

    def sources(self, me):
        first = jnp.where(me % 2 == 1, 4, 2)
        second = 6 - first
        zero = jnp.zeros_like(me)
        return me ^ jnp.stack(
            [zero, zero + 1, first, second, second + 1, first + 1, zero + 6, zero + 7]
        )

    def first_hop(self, block):
        return lax.ppermute(block, "expert", self.first)

    def far(self, first_block):
        return lax.ppermute(first_block, "expert", self.second)

    def to_mate(self, block):
        return lax.ppermute(block, "expert", self.mate)


class PlainExchange:
    def __init__(self, count):
        self.count = count

    def sources(self, me):
        return jnp.arange(self.count, dtype=jnp.int32)

    def gather(self, block):
        return lax.all_gather(block, "expert", tiled=True)

    def reduce(self, partial):
        return lax.psum_scatter(
            partial.astype(BF16), "expert", scatter_dimension=0, tiled=True
        ).astype(F32)


def local(
    tokens,
    cotangent,
    gate_weights,
    expert_ids,
    copy_pick,
    copy_expert,
    up_weight,
    down_weight,
    copy_up,
    copy_down,
):
    device_count = lax.axis_size("expert")
    me = lax.axis_index("expert")
    rows, width = tokens.shape
    chosen = expert_ids.shape[1]
    local_count = up_weight.shape[0]
    hidden = up_weight.shape[2]
    expert_count = local_count * device_count
    moved_most = 3 * (rows * chosen // expert_count) // 8
    moved_rows = padded(device_count * moved_most, 128)

    column_count = expert_count + device_count
    owner = expert_ids // local_count
    column = jnp.where(copy_pick == 1, expert_count + owner, expert_ids)
    hit = column[:, :, None] == jnp.arange(column_count, dtype=jnp.int32)
    gates = jnp.sum(jnp.where(hit, gate_weights[:, :, None], 0.0), axis=1)
    moved = jnp.sum(hit[:, :, expert_count:].astype(F32), axis=1)
    lower = (
        jnp.arange(rows, dtype=jnp.int32)[:, None] >= jnp.arange(rows, dtype=jnp.int32)[None, :]
    )
    rank = dot(lower.astype(BF16), moved.astype(BF16), (1, 0)) * moved
    gate_high, gate_low = split_two(gates)
    table_width = padded(2 * column_count + device_count, 128)
    table = jnp.concatenate(
        [
            gate_high,
            gate_low,
            rank.astype(BF16),
            jnp.zeros((rows, table_width - 2 * column_count - device_count), BF16),
        ],
        axis=1,
    )
    behind = (me + device_count - 1) % device_count
    columns = [local_count * me + i for i in range(local_count)] + [expert_count + behind]
    slots = len(columns)
    table_rows = jnp.arange(table_width, dtype=jnp.int32)
    wanted = jnp.stack(columns)
    high_pick = (table_rows[:, None] == wanted[None, :]).astype(BF16)
    low_pick = (table_rows[:, None] == wanted[None, :] + column_count).astype(BF16)
    wanted_rank = 2 * column_count + jnp.stack([behind, me])
    rank_pick = (table_rows[:, None] == wanted_rank[None, :]).astype(BF16)
    to_owner = [(i, (i - 1) % device_count) for i in range(device_count)]
    hot_slot = copy_expert[(me + 1) % device_count] % local_count
    own_width = local_count * hidden

    def finish(output_sum, gradient_sum, table_sum):
        grads = table_sum[:, :column_count] + table_sum[:, column_count : 2 * column_count]
        gate_grad = jnp.sum(jnp.where(hit, grads[:, None, :], 0.0), axis=2)
        return output_sum.astype(BF16), gradient_sum.astype(BF16), gate_grad

    replicas = lax.axis_size("dp")
    if device_count == 8 and local_count == 2 and replicas == 4:
        exchange = CubeExchange()
        replica = lax.axis_index("dp")
        hot = hot_slot.reshape(1).astype(jnp.int32)
        cold_column = local_count * me + 1 - hot_slot
        weights = (up_weight, down_weight, copy_up, copy_down)
        base = jnp.repeat((exchange.sources(me) * moved_most).astype(F32), rows)[None, :]
        slot_columns = jnp.stack([wanted[slots - 1], wanted[0], wanted[1]])
        pick_columns = jnp.stack(
            [wanted[slots - 1], wanted[0], wanted[1], wanted_rank[0], wanted_rank[1], cold_column]
            + [jnp.int32(-1)] * 10
        )
        is_gate = jnp.array([1, 1, 1, 0, 0, 1] + [0] * 10, jnp.int32)
        pick = (
            (table_rows[None, :] == pick_columns[:, None])
            | (
                (table_rows[None, :] == pick_columns[:, None] + column_count)
                & (is_gate[:, None] == 1)
            )
        ).astype(BF16)
        part_columns = jnp.stack(
            [slot_columns, slot_columns + column_count] + [jnp.full((slots,), -1, jnp.int32)] * 14,
            axis=1,
        ).reshape(-1)
        part_pick = (table_rows[None, :] == part_columns[:, None]).astype(BF16)

        own = jnp.concatenate([tokens, cotangent, table], axis=1)
        own_mate = exchange.to_mate(own)
        a, b = exchange.first_hop(own), exchange.far(own)
        replica_pairs = [(0, 1), (1, 0), (2, 3), (3, 2)]
        other = lax.ppermute(own, "dp", replica_pairs)
        blocks_1 = [own, own_mate]
        ends = (2 * rows, 6 * rows)
        grad_1, active_1, part_1, place_1, packed = hidden_call(
            hot, blocks_1, weights, pick, base[:, : ends[0]], (COPY, 0, 1), moved_rows
        )
        a, b, grad_1 = lax.optimization_barrier((a, b, grad_1))
        d = exchange.far(a)
        a_mate = exchange.to_mate(a)
        other, a_mate = lax.optimization_barrier((other, a_mate))
        blocks_2 = [a, b, a_mate, exchange.to_mate(b)]
        grad_2, active_2, part_2, place_2, packed = hidden_call(
            hot, blocks_2, weights, pick, base[:, ends[0] : ends[1]], (COPY, 0, 1), moved_rows,
            packed,
        )
        grad_2, d = lax.optimization_barrier((grad_2, d))
        blocks_3 = [d, exchange.to_mate(d)]
        blocks = blocks_1 + blocks_2 + blocks_3

        other_a = exchange.first_hop(other)

        late_base = base[:, ends[1] :]
        grad_copy, active_copy, part_copy, place_3, packed = hidden_call(
            hot, blocks_3, weights, pick, late_base, (COPY,), moved_rows, packed
        )
        packed = lax.ppermute(packed, "expert", to_owner)
        grad_3, active_3, part_3 = hidden_call(hot, blocks_3, weights, pick, late_base, (0, 1))
        packed, grad_3, other, other_a = lax.optimization_barrier(
            (packed, grad_3, other, other_a)
        )
        other_b = exchange.far(other)
        other_d = exchange.far(other_a)
        hot_grads = hot_call(
            hot, blocks, (1, 1, 0), (grad_1, grad_2, grad_3), (active_1, active_2, active_3),
            (place_1, place_2, place_3), packed, width, replicas,
        )
        hot_sum = lax.psum_scatter(hot_grads, "dp", scatter_dimension=0, tiled=True)[0]

        grad_3, active_3, _ = lax.optimization_barrier((grad_3, active_3, hot_grads))
        sides = (
            (grad_1, grad_2, grad_copy, grad_3),
            (active_1, active_2, active_copy, active_3),
            (part_1, part_2, part_copy, part_3),
            weights, part_pick,
        )
        mates_rows = rows_call(1, *sides)
        *mates_rows, other_b = lax.optimization_barrier((*mates_rows, other_b))
        arrived = [exchange.to_mate(block) for block in mates_rows]
        own_rows = rows_call(0, *sides, tuple(arrived))
        gradient_rows, output_rows = own_rows[:4], own_rows[4:]
        other_d, _ = lax.optimization_barrier((other_d, own_rows[0]))
        pair_blocks = [other, other_a, other_b, other_d]
        pair_blocks = pair_blocks + [exchange.to_mate(block) for block in pair_blocks]
        from_diagonal = [exchange.far(rows_of[3]) for rows_of in (gradient_rows, output_rows)]
        grad_pair, active_pair = hidden_call(hot, pair_blocks, weights, pick, base, (COLD,))
        grad_pair, *from_diagonal = lax.optimization_barrier((grad_pair, *from_diagonal))
        chunk_pairs = jnp.array([[1, 0], [3, 2], [0, 1], [2, 3]], jnp.int32)
        given, second = cold_call(
            hot, chunk_pairs[replica], blocks + pair_blocks, (1, 1, 0, None),
            (grad_1, grad_2, grad_3, grad_pair), (active_1, active_2, active_3, active_pair),
            width, width // replicas,
        )
        at_end = (replica == 0) | (replica == replicas - 1)
        flags = jnp.stack([hot_slot, at_end.astype(jnp.int32)]).astype(jnp.int32)
        filled = place_call(flags, [hot_sum])
        *from_diagonal, first_filled = lax.optimization_barrier((*from_diagonal, filled[0]))
        filled = (first_filled, filled[1])
        relayed = [
            (rows_of[1].astype(F32) + arrived.astype(F32)).astype(BF16)
            for rows_of, arrived in zip((gradient_rows, output_rows), from_diagonal)
        ]
        moved = lax.ppermute(given, "dp", [(0, 1), (1, 3), (2, 0), (3, 2)])
        hops = [exchange.far(rows_of[2]) for rows_of in (gradient_rows, output_rows)]
        gradient_hop, output_hop = (exchange.first_hop(block) for block in relayed)
        moved, to_middle, gradient_hop, *hops = lax.optimization_barrier(
            (moved, second, gradient_hop, *hops)
        )
        gradient_sum, output_sum = (
            rows_of[0].astype(F32) + first.astype(F32) + other_hop.astype(F32)
            for rows_of, first, other_hop in zip(
                (gradient_rows, output_rows), (gradient_hop, output_hop), hops
            )
        )
        across = lax.ppermute(to_middle, "dp", [(1, 2), (2, 1)])
        up_grad, down_grad = place_call(flags, [moved, second, across], filled)
        return (*finish(output_sum[:, :width], gradient_sum, output_sum[:, width:]), up_grad, down_grad)

    exchange = PlainExchange(device_count)
    up_all = jnp.concatenate([up_weight[i] for i in range(local_count)] + [copy_up[0]], axis=1)
    down_all = jnp.concatenate(
        [down_weight[i] for i in range(local_count)] + [copy_down[0]], axis=0
    )

    def some_rows(own_block):
        gathered = exchange.gather(own_block)
        all_tokens = gathered[:, :width]
        all_cotangent = gathered[:, width : 2 * width]
        all_table = gathered[:, 2 * width :]
        slot_gates = dot(all_table, high_pick + low_pick, (1, 0))
        ranks = dot(all_table, rank_pick, (1, 0)).astype(jnp.int32)
        base = jnp.repeat(exchange.sources(me) * moved_most, own_block.shape[0])
        place = jnp.where(ranks > 0, base[:, None] + ranks - 1, -1)
        moved_index = jnp.arange(moved_rows, dtype=jnp.int32)[None, :]
        served_place = (place[:, :1] == moved_index).astype(BF16)
        owned_place = (place[:, 1:] == moved_index).astype(BF16)
        linear = dot(all_tokens, up_all, (1, 0))
        raw_grad = dot(all_cotangent, down_all, (1, 1))
        spread = jnp.repeat(slot_gates, hidden, axis=1)
        sigma = jax.nn.sigmoid(linear)
        active = (linear * sigma).astype(BF16).astype(F32)
        gate_part = jnp.sum((active * raw_grad).reshape(-1, slots, hidden), axis=2)
        weighted = (spread * active).astype(BF16)
        slope = sigma * (1.0 + linear * (1.0 - sigma))
        linear_grad = (spread * raw_grad * slope).astype(BF16)
        both = jnp.concatenate([linear_grad[:, own_width:], weighted[:, own_width:]], axis=1)
        packed = dot(served_place, both, (0, 0)).astype(BF16)
        packed = lax.ppermute(packed, "expert", to_owner)
        unpacked = dot(owned_place, packed, (1, 0)).astype(BF16)
        up_parts = []
        down_parts = []
        for i in range(local_count):
            here = (hot_slot == i).astype(BF16)
            part = slice(i * hidden, (i + 1) * hidden)
            total_grad = linear_grad[:, part] + unpacked[:, :hidden] * here
            total_active = weighted[:, part] + unpacked[:, hidden:] * here
            up_parts.append(dot(all_tokens, total_grad, (0, 0)))
            down_parts.append(dot(total_active, all_cotangent, (0, 0)))
        mixed = dot(weighted, down_all, (1, 0)).astype(BF16)
        back = dot(linear_grad, up_all, (1, 1)).astype(BF16)
        part_high, part_low = split_two(gate_part)
        grad_table = dot(part_high, high_pick, (1, 1)) + dot(part_low, low_pick, (1, 1))
        summed = exchange.reduce(
            jnp.concatenate([mixed, back, grad_table.astype(BF16)], axis=1)
        )
        return summed, jnp.stack(up_parts), jnp.stack(down_parts)

    own = jnp.concatenate([tokens, cotangent, table], axis=1)
    pieces = max(1, device_count // 8)
    if pieces == 1:
        summed, up_sum, down_sum = some_rows(own)
    else:

        def step(totals, piece):
            summed, up_part, down_part = some_rows(piece)
            return (totals[0] + up_part, totals[1] + down_part), summed

        zeros = (jnp.zeros(up_weight.shape, F32), jnp.zeros(down_weight.shape, F32))
        (up_sum, down_sum), summed = lax.scan(
            step, zeros, own.reshape(pieces, rows // pieces, own.shape[1])
        )
        summed = summed.reshape(rows, own.shape[1])
    up_grad = lax.psum_scatter(up_sum.astype(BF16), "dp", scatter_dimension=1, tiled=True)
    down_grad = lax.psum_scatter(down_sum.astype(BF16), "dp", scatter_dimension=2, tiled=True)
    parts = (summed[:, :width], summed[:, width : 2 * width], summed[:, 2 * width :])
    return (*finish(*parts), up_grad, down_grad)


def solution(mesh):
    placed = (
        P(("expert", "dp"), None),
        P(("expert", "dp"), None),
        P(("expert", "dp"), None),
        P(("expert", "dp"), None),
        P(("expert", "dp"), None),
        P(),
        P("expert", None, None),
        P("expert", None, None),
        P("expert", None, None),
        P("expert", None, None),
    )
    return jax.shard_map(
        local,
        mesh=mesh,
        in_specs=placed,
        out_specs=(
            P(("expert", "dp"), None),
            P(("expert", "dp"), None),
            P(("expert", "dp"), None),
            P("expert", "dp", None),
            P("expert", None, "dp"),
        ),
        check_vma=False,
    )
```
